256 devices in a mesh: ctx: 32 (over z_hi, y, x), tp: 8 (over z_lo, core).
Axes of the slice: x: 4, y: 4, z: 8 (z_hi: 2, z_lo: 4; z = z_hi * 4 + z_lo), core: 2. Of those that a mesh axis runs over, the one named last changes fastest.
Arguments:
- query_window: bfloat16 [512, 8192], P(None, 'tp'), may hold values from -200 to 200
- key_cache: bfloat16 [16384, 512], P('ctx'), may hold values from -8 to 8
- value_cache: bfloat16 [16384, 512], P('ctx'), may hold values from -6 to 6
- out_weight: bfloat16 [8192, 4096], P('tp'), may hold values from -0.09375 to 0.09375
- grad_routed: bfloat16 [512, 4096], P('ctx', 'tp'), may hold values from -6 to 6
- token_route: int32 [512], replicated, may hold values from 0 to 511, each once
- window_start: int32 [1], replicated, may hold values from 8192 to 15872
Outputs:
- grad_query: bfloat16 [512, 8192], P('ctx', 'tp')
- grad_keys: bfloat16 [16384, 512], P(('ctx', 'tp'))
- grad_values: bfloat16 [16384, 512], P(('ctx', 'tp'))
The draws below stay inside these ranges and needn't reach their ends.
Inputs may be any that keep to these rules, and one draw needn't show every extreme that they name: `token_route`: each window token appears once.
All inputs are finite; a program needn't handle non-finite values.
Results may differ from the reference program's by a relative error of at most 0.012.
Values may be sent and summed in bfloat16 or wider, within the bound.
No kernel may reach another device: no remote copies, remote signals or barrier semaphores. Data moves between devices by JAX's collectives and lax.ppermute only.
A program may use at most 320 MiB of HBM per device.

```python
import math
import jax
import jax.numpy as jnp
from jax import lax

D = 4096
HQ = 64
KVH = 4
HD = 128
Q = 512
CTX_LEN = 16384


def cache_keys(key):
    drawn = jnp.clip(jax.random.normal(jax.random.fold_in(key, 11), (CTX_LEN, KVH * HD), jnp.float32), -6.0, 6.0)
    return drawn


def draw_key_cache(key, part):
    return jnp.clip(cache_keys(key), -8.0, 8.0).astype(jnp.bfloat16)


def draw_query_window(key, part):
    drawn = jnp.clip(jax.random.normal(jax.random.fold_in(key, 12), (Q, HQ * HD), jnp.float32), -6.0, 6.0)
    return jnp.clip(drawn, -200.0, 200.0).astype(jnp.bfloat16)


def levels(rng, dims, cuts, smallest, largest):
    level, own = 1.0, jax.random.fold_in(rng, 6)
    for position, parts in cuts:
        steps = jnp.exp(jax.random.uniform(jax.random.fold_in(own, position), (parts,), jnp.float32, smallest / len(cuts), largest / len(cuts)))
        level = level * jnp.repeat(steps, dims[position] // parts).reshape([-1 if axis == position else 1 for axis in range(len(dims))])
    return level


def bell_draw(key, dims, scale, reach, shards=(), held_as=jnp.bfloat16):
    loudness = levels(key, dims, shards, -0.22, 0.18) if shards else 1.0
    values = jax.random.normal(key, dims, jnp.float32) * scale * loudness
    return jnp.minimum(jnp.maximum(values, -reach), reach).astype(held_as)


def setup_inputs(seed: int = 0) -> dict:
    keys = jax.random.split(jax.random.key(seed), 8)
    return {
        "query_window": draw_query_window(jax.random.fold_in(keys[7], 71), 0),
        "key_cache": draw_key_cache(jax.random.fold_in(keys[7], 71), 0),
        "value_cache": bell_draw(keys[2], (CTX_LEN, KVH * HD), 1.0, 6.0, ((0, 32),)),
        "out_weight": bell_draw(keys[3], (HQ * HD, D), D ** -0.5, 0.09375, ((0, 8),)),
        "grad_routed": bell_draw(keys[4], (Q, D), 1.0, 6.0, ((0, 32), (1, 8))),
        "token_route": jax.random.permutation(keys[5], Q).astype(jnp.int32),
        "window_start": jax.random.randint(keys[6], (1,), CTX_LEN // 2, CTX_LEN - Q + 1).astype(jnp.int32),
    }


NEG_FILL = -1e+30

def reference(query_window, key_cache, value_cache, out_weight, grad_routed, token_route, window_start):
    group_size = HQ // KVH
    scale_factor = 1.0 / math.sqrt(HD)
    highest = lax.Precision.HIGHEST
    token_grad = jnp.zeros((Q, D), jnp.bfloat16).at[token_route].set(grad_routed)
    head_grad = jnp.dot(token_grad, out_weight.T, preferred_element_type=jnp.float32).astype(jnp.bfloat16)
    query_pos = window_start[0] + jnp.arange(Q, dtype=jnp.int32)
    key_pos = jnp.arange(CTX_LEN, dtype=jnp.int32)
    visible = key_pos[None, :] <= query_pos[:, None]
    query_parts = []
    key_parts = []
    value_parts = []
    for kv_head in range(KVH):
        key_head = key_cache[:, kv_head * HD:(kv_head + 1) * HD].astype(jnp.float32)
        value_head = value_cache[:, kv_head * HD:(kv_head + 1) * HD].astype(jnp.float32)

        def one_head(accums, head_index):
            col_start = (head_index * HD).astype(jnp.int32)
            query_head = lax.dynamic_slice_in_dim(query_window, col_start, HD, 1).astype(jnp.float32)
            grad_head = lax.dynamic_slice_in_dim(head_grad, col_start, HD, 1).astype(jnp.float32)
            scores = jnp.dot(query_head, key_head.T, precision=highest) * scale_factor
            scores = jnp.where(visible, scores, NEG_FILL)
            row_peak = lax.optimization_barrier(jnp.max(scores, axis=1, keepdims=True))
            weights = jnp.where(visible, jnp.exp(scores - row_peak), 0.0)
            attn_probs = weights / lax.optimization_barrier(jnp.sum(weights, axis=1, keepdims=True))
            grad_probs = jnp.dot(grad_head, value_head.T, precision=highest)
            row_delta = lax.optimization_barrier(jnp.sum(attn_probs * grad_probs, axis=1, keepdims=True))
            score_grad = lax.optimization_barrier((attn_probs * (grad_probs - row_delta)).astype(jnp.bfloat16)).astype(jnp.float32)
            probs_half = lax.optimization_barrier(attn_probs.astype(jnp.bfloat16)).astype(jnp.float32)
            grad_query = (scale_factor * jnp.dot(score_grad, key_head, precision=highest)).astype(jnp.bfloat16)
            key_accum = accums[0] + jnp.dot(score_grad.T, query_head, precision=highest)
            value_accum = accums[1] + jnp.dot(probs_half.T, grad_head, precision=highest)
            return ((key_accum, value_accum), grad_query)
        zero_block = jnp.zeros((CTX_LEN, HD), jnp.float32)
        head_ids = jnp.arange(group_size, dtype=jnp.int32) + kv_head * group_size
        (key_accum, value_accum), per_head = lax.scan(one_head, (zero_block, zero_block), head_ids)
        query_parts.append(jnp.transpose(per_head, (1, 0, 2)).reshape(Q, group_size * HD))
        key_parts.append((scale_factor * key_accum).astype(jnp.bfloat16))
        value_parts.append(value_accum.astype(jnp.bfloat16))
    return (jnp.concatenate(query_parts, axis=1), jnp.concatenate(key_parts, axis=1), jnp.concatenate(value_parts, axis=1))
```

```python
import functools
import math

import jax
import jax.numpy as jnp
from jax import lax
from jax.experimental import pallas as pl
from jax.experimental.pallas import tpu as pltpu
from jax.sharding import Mesh
from jax.sharding import PartitionSpec as P

HQ = 64
KVH = 4
HD = 128
GROUP = HQ // KVH
SCALE = 1.0 / math.sqrt(HD)
NEG = -1e30
FLOOR = -1e29
LINE = ("zh", "tp")

BF = jnp.bfloat16
F32 = jnp.float32
ROWS = (((1,), (1,)), ((), ()))


def dot(a, b, dims=None):
    if dims is None:
        return jnp.dot(a, b, preferred_element_type=F32)
    return lax.dot_general(a, b, dims, preferred_element_type=F32)


def params(mib):
    return pltpu.CompilerParams(
        vmem_limit_bytes=mib * 1024 * 1024, dimension_semantics=("arbitrary",)
    )


def project_kernel(grad_ref, weight_ref, out_ref, total):
    step = pl.program_id(0)

    @pl.when(step == 0)
    def _():
        total[...] = jnp.zeros_like(total)

    rows = grad_ref.shape[0] * grad_ref.shape[2]
    total[...] += dot(grad_ref[...].reshape(rows, grad_ref.shape[3]), weight_ref[...], ROWS)

    @pl.when(step == pl.num_programs(0) - 1)
    def _():
        out_ref[...] = total[...].astype(BF)


def project(grads, weight):
    lines, parts, rows, width = grads.shape
    heads = weight.shape[0]
    return pl.pallas_call(
        project_kernel,
        grid=(parts,),
        in_specs=[
            pl.BlockSpec((lines, 1, rows, width), lambda i: (0, i, 0, 0)),
            pl.BlockSpec((heads, width), lambda i: (0, i)),
        ],
        out_specs=pl.BlockSpec((lines * rows, heads), lambda i: (0, 0)),
        out_shape=jax.ShapeDtypeStruct((lines * rows, heads), BF),
        scratch_shapes=[pltpu.VMEM((lines * rows, heads), F32)],
        compiler_params=params(24),
        name="project",
    )(grads, weight)


def scores_kernel(place, query_ref, own_ref, other_ref, expo_ref, peak_ref, total_ref):
    head = pl.program_id(0)
    query = query_ref[...]
    span, window = own_ref.shape[0], query.shape[0]
    query_pos = (
        place[3] + place[0] * window + lax.broadcasted_iota(jnp.int32, (1, window), 1)
    )
    scored = []
    for slot, keys in enumerate((own_ref, other_ref)):
        key_pos = place[1 + slot] + lax.broadcasted_iota(jnp.int32, (span, 1), 0)
        raw = dot(keys[...], query, ROWS) * (SCALE * math.log2(math.e))
        scored.append(jnp.where(key_pos <= query_pos, raw, NEG))
    peak = jnp.maximum(
        jnp.max(scored[0], axis=0, keepdims=True), jnp.max(scored[1], axis=0, keepdims=True)
    )
    peak = jnp.maximum(peak, FLOOR)
    total = jnp.zeros_like(peak)
    for slot in range(2):
        expo = jnp.exp2(scored[slot] - peak)
        expo_ref[0, slot] = expo
        total += jnp.sum(expo, axis=0, keepdims=True)
    peak_ref[pl.ds(head, 1), :] = peak
    total_ref[pl.ds(head, 1), :] = total


def scores(place, queries, key_cache, others, half, local_heads):
    span = key_cache.shape[0]
    return pl.pallas_call(
        scores_kernel,
        grid_spec=pltpu.PrefetchScalarGridSpec(
            num_scalar_prefetch=1,
            grid=(local_heads,),
            in_specs=[
                pl.BlockSpec((half, HD), lambda h, p: (p[0], h)),
                pl.BlockSpec((span, HD), lambda h, p: (0, p[4])),
                pl.BlockSpec((span, HD), lambda h, p: (0, 0)),
            ],
            out_specs=[
                pl.BlockSpec((1, 2, span, half), lambda h, p: (h, 0, 0, 0)),
                pl.BlockSpec((local_heads, half), lambda h, p: (0, 0)),
                pl.BlockSpec((local_heads, half), lambda h, p: (0, 0)),
            ],
        ),
        out_shape=[
            jax.ShapeDtypeStruct((local_heads, 2, span, half), F32),
            jax.ShapeDtypeStruct((local_heads, half), F32),
            jax.ShapeDtypeStruct((local_heads, half), F32),
        ],
        compiler_params=params(24),
        cost_estimate=pl.CostEstimate(
            flops=2 * local_heads * 2 * span * half * HD,
            bytes_accessed=4 * local_heads * 2 * span * half,
            transcendentals=local_heads * 2 * span * half,
        ),
        name="scores",
    )(place, queries, key_cache, others)


def delta_kernel(place, route_ref, grad_ref, own_ref, other_ref, expo_ref, out_ref, delta_ref):
    head = pl.program_id(0)
    half, window = out_ref.shape[0], grad_ref.shape[0] * grad_ref.shape[1]
    token = place[0] * half + lax.broadcasted_iota(jnp.int32, (half, window), 0)
    pick = jnp.where(route_ref[...] == token, 1.0, 0.0).astype(BF)
    grad = dot(pick, grad_ref[...].reshape(window, HD)).astype(BF)
    out_ref[...] = grad
    delta = jnp.zeros((1, half), F32)
    for slot, values in enumerate((own_ref, other_ref)):
        delta += jnp.sum(expo_ref[0, slot] * dot(values[...], grad, ROWS), axis=0, keepdims=True)
    delta_ref[pl.ds(head, 1), :] = delta


def deltas(place, route, grads, value_cache, others, expo):
    local_heads, _, span, half = expo.shape
    groups, rows, width = grads.shape
    return pl.pallas_call(
        delta_kernel,
        grid_spec=pltpu.PrefetchScalarGridSpec(
            num_scalar_prefetch=1,
            grid=(local_heads,),
            in_specs=[
                pl.BlockSpec((1, groups * rows), lambda h, p: (0, 0)),
                pl.BlockSpec((groups, rows, HD), lambda h, p: (0, 0, h)),
                pl.BlockSpec((span, HD), lambda h, p: (0, p[4])),
                pl.BlockSpec((span, HD), lambda h, p: (0, 1)),
                pl.BlockSpec((1, 2, span, half), lambda h, p: (h, 0, 0, 0)),
            ],
            out_specs=[
                pl.BlockSpec((half, HD), lambda h, p: (0, h)),
                pl.BlockSpec((local_heads, half), lambda h, p: (0, 0)),
            ],
        ),
        out_shape=[
            jax.ShapeDtypeStruct((half, width), BF),
            jax.ShapeDtypeStruct((local_heads, half), F32),
        ],
        compiler_params=params(24),
        name="deltas",
    )(place, route, grads, value_cache, others, expo)


def grads_kernel(
    place,
    stats_ref,
    peak_ref,
    query_ref,
    grad_ref,
    key_own,
    key_other,
    value_own,
    value_other,
    expo_ref,
    query_out,
    cache_out,
    factor,
    delta,
    keys_turned,
    key_total,
    value_total,
):
    head = pl.program_id(0)

    @pl.when(head == 0)
    def _():
        peaks = stats_ref[:, 0]
        peak = jnp.max(peaks, axis=0)
        weight = jnp.exp2(peaks - peak[None])
        total = jnp.sum(weight * stats_ref[:, 1], axis=0)
        factor[...] = jnp.exp2(peak_ref[...] - peak) / total
        delta[...] = jnp.sum(weight * stats_ref[:, 2], axis=0) / total
        for slot, keys in enumerate((key_own, key_other)):
            keys_turned[slot] = keys[...].astype(F32).T.astype(BF)
        key_total[...] = jnp.zeros_like(key_total)
        value_total[...] = jnp.zeros_like(value_total)

    query, grad = query_ref[...], grad_ref[...]
    row_factor, row_delta = factor[pl.ds(head, 1), :], delta[pl.ds(head, 1), :]
    turned = jnp.zeros((HD, query.shape[0]), F32)
    for slot, values in enumerate((value_own, value_other)):
        probs = expo_ref[0, slot] * row_factor
        score_grad = (probs * (dot(values[...], grad, ROWS) - row_delta)).astype(BF)
        value_total[slot] += dot(probs.astype(BF), grad)
        key_total[slot] += dot(score_grad, query)
        turned += dot(keys_turned[slot], score_grad)
    query_out[...] = (SCALE * turned).T.astype(BF)

    @pl.when(head == pl.num_programs(0) - 1)
    def _():
        parts, rows = cache_out.shape[0] // 2, cache_out.shape[1]
        for slot in range(2):
            line = place[0] if slot == 0 else 1 - place[0]
            where = pl.ds(line * parts, parts)
            cache_out[where, :, :HD] = (
                (SCALE * key_total[slot]).astype(BF).reshape(parts, rows, HD)
            )
            cache_out[where, :, HD:] = value_total[slot].astype(BF).reshape(parts, rows, HD)


def gradients(place, stats, peak, queries, grads, key_cache, value_cache, others, expo, parts):
    local_heads, _, span, half = expo.shape
    groups = stats.shape[0]
    return pl.pallas_call(
        grads_kernel,
        grid_spec=pltpu.PrefetchScalarGridSpec(
            num_scalar_prefetch=1,
            grid=(local_heads,),
            in_specs=[
                pl.BlockSpec((groups, 3, local_heads, half), lambda h, p: (0, 0, 0, 0)),
                pl.BlockSpec((local_heads, half), lambda h, p: (0, 0)),
                pl.BlockSpec((half, HD), lambda h, p: (p[0], h)),
                pl.BlockSpec((half, HD), lambda h, p: (0, h)),
                pl.BlockSpec((span, HD), lambda h, p: (0, p[4])),
                pl.BlockSpec((span, HD), lambda h, p: (0, 0)),
                pl.BlockSpec((span, HD), lambda h, p: (0, p[4])),
                pl.BlockSpec((span, HD), lambda h, p: (0, 1)),
                pl.BlockSpec((1, 2, span, half), lambda h, p: (h, 0, 0, 0)),
            ],
            out_specs=[
                pl.BlockSpec((half, HD), lambda h, p: (0, h)),
                pl.BlockSpec((2 * parts, span // parts, 2 * HD), lambda h, p: (0, 0, 0)),
            ],
            scratch_shapes=[
                pltpu.VMEM((local_heads, half), F32),
                pltpu.VMEM((local_heads, half), F32),
                pltpu.VMEM((2, HD, span), BF),
                pltpu.VMEM((2, span, HD), F32),
                pltpu.VMEM((2, span, HD), F32),
            ],
        ),
        out_shape=[
            jax.ShapeDtypeStruct((half, local_heads * HD), BF),
            jax.ShapeDtypeStruct((2 * parts, span // parts, 2 * HD), BF),
        ],
        compiler_params=params(32),
        name="gradients",
    )(
        place,
        stats,
        peak,
        queries,
        grads,
        key_cache,
        others,
        value_cache,
        others,
        expo,
    )


def to_all(value, axis, count):
    return lax.all_to_all(jnp.broadcast_to(value[None], (count,) + value.shape), axis, 0, 0)


def on_device(
    lines,
    groups,
    parts,
    query_window,
    key_cache,
    value_cache,
    out_weight,
    grad_routed,
    token_route,
    window_start,
):
    window, local_heads = query_window.shape[0], query_window.shape[1] // HD
    half, span, rows = window // lines, key_cache.shape[0], grad_routed.shape[0]
    line, group, part = lax.axis_index("zh"), lax.axis_index("xy"), lax.axis_index("tp")
    kv_head = part * local_heads // GROUP
    first = (line * groups + group) * span
    first_other = ((1 - line) * groups + group) * span
    place = jnp.stack([line, first, first_other, window_start[0], kv_head]).astype(jnp.int32)

    with jax.named_scope("gradient_rows"):
        rows_in = to_all(grad_routed, LINE, lines * parts)
        rows_in = rows_in.reshape(lines, parts, rows, grad_routed.shape[1])
    with jax.named_scope("cache_pair"):
        mine = jnp.concatenate(
            [
                lax.dynamic_slice_in_dim(key_cache, kv_head * HD, HD, 1),
                lax.dynamic_slice_in_dim(value_cache, kv_head * HD, HD, 1),
            ],
            axis=1,
        )
        others = lax.ppermute(mine, "zh", [(0, 1), (1, 0)])
    head_grad = project(rows_in, out_weight)
    with jax.named_scope("head_gradients"):
        gathered = to_all(head_grad, "xy", groups)
    expo, peak, total = scores(place, query_window, key_cache, others, half, local_heads)
    route = token_route.reshape(lines, groups, rows).transpose(1, 0, 2).reshape(1, window)
    grads, delta = deltas(place, route, gathered, value_cache, others, expo)
    with jax.named_scope("row_stats"):
        stats = to_all(jnp.stack([peak, total, delta]), "xy", groups)
    query_part, cache_part = gradients(
        place, stats, peak, query_window, grads, key_cache, value_cache, others, expo, parts
    )
    with jax.named_scope("query_terms"):
        query_terms = lax.all_to_all(
            query_part.reshape(groups, half // groups, query_part.shape[1]), "xy", 0, 0
        )
        grad_query = jnp.sum(query_terms.astype(F32), axis=0).astype(BF)
    with jax.named_scope("cache_terms"):
        cache_terms = lax.all_to_all(cache_part, LINE, 0, 0)
        per_head = parts // KVH
        share = cache_terms.shape[1]
        cache_sum = jnp.sum(
            cache_terms.reshape(lines, KVH, per_head, share, 2, HD).astype(F32), axis=(0, 2)
        ).astype(BF)
        grad_keys = cache_sum[:, :, 0].transpose(1, 0, 2).reshape(share, KVH * HD)
        grad_values = cache_sum[:, :, 1].transpose(1, 0, 2).reshape(share, KVH * HD)
    return grad_query, grad_keys, grad_values


def solution(mesh):
    lines = 2
    groups, parts = mesh.shape["ctx"] // lines, mesh.shape["tp"]
    fine = Mesh(mesh.devices.reshape(lines, groups, parts), ("zh", "xy", "tp"))
    ctx = ("zh", "xy")
    in_specs = (
        P(None, "tp"),
        P(ctx, None),
        P(ctx, None),
        P("tp", None),
        P(ctx, "tp"),
        P(),
        P(),
    )
    out_specs = (P(ctx, "tp"), P(ctx + ("tp",), None), P(ctx + ("tp",), None))
    return jax.shard_map(
        functools.partial(on_device, lines, groups, parts),
        mesh=fine,
        in_specs=in_specs,
        out_specs=out_specs,
        check_vma=False,
    )
```

```python
import functools
import math

import jax
import jax.numpy as jnp
from jax import lax
from jax.experimental import pallas as pl
from jax.experimental.pallas import tpu as pltpu
from jax.sharding import Mesh
from jax.sharding import PartitionSpec as P

HQ = 64
KVH = 4
HD = 128
GROUP = HQ // KVH
SCALE = 1.0 / math.sqrt(HD)
NEG = -1e30
FLOOR = -1e29
VMEM_MIB = 16
LOG2E = math.log2(math.e)

BF = jnp.bfloat16
F32 = jnp.float32
ROWS = (((1,), (1,)), ((), ()))


def dot(a, b, dims=None):
    if dims is None:
        return jnp.dot(a, b, preferred_element_type=F32)
    return lax.dot_general(a, b, dims, preferred_element_type=F32)


VMEM = pl.BlockSpec(memory_space=pltpu.VMEM)
SMEM = pl.BlockSpec(memory_space=pltpu.SMEM)


HBM = pl.BlockSpec(memory_space=pltpu.HBM)


def call(kernel, name, args, outs, scratch=(), cost=None, streamed=(), held=()):
    return pl.pallas_call(
        kernel,
        in_specs=[SMEM] + [HBM if i in streamed else VMEM for i in range(1, len(args))],
        out_specs=[VMEM] * len(outs),
        out_shape=[
            pltpu.VMEM(*out) if i in held else jax.ShapeDtypeStruct(*out)
            for i, out in enumerate(outs)
        ],
        scratch_shapes=list(scratch),
        compiler_params=pltpu.CompilerParams(vmem_limit_bytes=VMEM_MIB * 1024 * 1024),
        cost_estimate=cost,
        name=name,
    )(*args)


def in_hbm(array):
    return pltpu.with_memory_space_constraint(array, pltpu.HBM)


def in_vmem(array):
    return pltpu.with_memory_space_constraint(array, pltpu.VMEM)


LINE, FIRST, FIRST_OTHER, START, KV_HEAD, CORE, BLOCKS = range(7)


def columns(index, width=HD):
    return pl.ds(pl.multiple_of(index * width, width), width)


def project_kernel(place, *refs):
    pieces, weight_ref, out_ref = refs[:-2], refs[-2], refs[-1]
    cores, lines, rows, width = pieces[0].shape
    total = None
    for index in range(len(pieces) * cores):
        piece = pieces[index // cores][index % cores].reshape(lines * rows, width)
        term = dot(weight_ref[:, columns(place[BLOCKS + index], width)], piece, ROWS)
        total = term if total is None else total + term
    result = total.T.astype(BF)
    for copy in range(out_ref.shape[0]):
        out_ref[copy] = result


def other_pair(place, straight, crossed):
    swap = place[CORE] == 1
    first, second = straight[...], crossed[...]
    return jnp.where(swap, second, first), jnp.where(swap, first, second)


def score_heads(place, slot, query_ref, keys, expo_ref, peak_ref, total_ref):
    heads, span, window = expo_ref.shape
    query_pos = place[START] + place[LINE] * window + lax.broadcasted_iota(jnp.int32, (1, window), 1)
    key_pos = place[FIRST + slot] + lax.broadcasted_iota(jnp.int32, (span, 1), 0)

    def one_head(head, _):
        query = query_ref[pl.ds(place[LINE] * window, window), columns(head)]
        scored = dot(keys, query, ROWS) * (SCALE * LOG2E)
        scored = jnp.where(key_pos <= query_pos, scored, NEG)
        peak = jnp.maximum(jnp.max(scored, axis=0, keepdims=True), FLOOR)
        expo = jnp.exp2(scored - peak)
        expo_ref[head] = expo
        peak_ref[pl.ds(head, 1), :] = peak
        total_ref[pl.ds(head, 1), :] = jnp.sum(expo, axis=0, keepdims=True)
        return 0

    lax.fori_loop(0, heads, one_head, 0)


def own_kernel(place, query_ref, key_ref, weight_in, expo_ref, peak_ref, total_ref, weight_out, done):
    copy = pltpu.make_async_copy(weight_in, weight_out, done)
    copy.start()
    keys = key_ref[:, columns(place[KV_HEAD])]
    score_heads(place, 0, query_ref, keys, expo_ref, peak_ref, total_ref)
    copy.wait()


def other_kernel(place, query_ref, straight, crossed, expo_ref, peak_ref, total_ref):
    keys = other_pair(place, straight, crossed)[0]
    score_heads(place, 1, query_ref, keys, expo_ref, peak_ref, total_ref)


def delta_kernel(
    place,
    route_ref,
    gathered_ref,
    value_ref,
    straight,
    crossed,
    expo_own,
    peak_own,
    total_own,
    expo_other,
    peak_other,
    total_other,
    grad_ref,
    stats_ref,
):
    heads, span, half = expo_own.shape
    window = route_ref.shape[1]
    token = place[LINE] * half + lax.broadcasted_iota(jnp.int32, (half, window), 0)
    pick = jnp.where(route_ref[...] == token, 1.0, 0.0).astype(BF)
    values = (value_ref[:, columns(place[KV_HEAD])], other_pair(place, straight, crossed)[1])
    grad_ref[...] = dot(pick, gathered_ref[...].reshape(window, heads * HD)).astype(BF)
    peak = jnp.maximum(peak_own[...], peak_other[...])
    factors = (jnp.exp2(peak_own[...] - peak), jnp.exp2(peak_other[...] - peak))
    stats_ref[0, 0] = peak
    stats_ref[0, 1] = total_own[...] * factors[0] + total_other[...] * factors[1]

    def one_head(head, _):
        grad = grad_ref[:, columns(head)]
        for slot, expo_ref in enumerate((expo_own, expo_other)):
            stats_ref[1 + slot, 2, pl.ds(head, 1), :] = jnp.sum(
                expo_ref[head] * dot(values[slot], grad, ROWS), axis=0, keepdims=True
            )
        return 0

    lax.fori_loop(0, heads, one_head, 0)
    stats_ref[0, 2] = stats_ref[1, 2] * factors[0] + stats_ref[2, 2] * factors[1]
    for copy in range(1, stats_ref.shape[0]):
        stats_ref[copy] = stats_ref[0]


def grads_kernel(
    place,
    stats_ref,
    query_ref,
    grad_ref,
    key_ref,
    value_ref,
    straight,
    crossed,
    expo_own,
    peak_own,
    expo_other,
    peak_other,
    query_out,
    keep_out,
    send_out,
    factor,
    delta,
    keys_turned,
    key_total,
    value_total,
):
    heads, span, half = expo_own.shape
    peaks = stats_ref[:, 0]
    peak = jnp.max(peaks, axis=0)
    weight = jnp.exp2(peaks - peak[None])
    total = jnp.sum(weight * stats_ref[:, 1], axis=0)
    for slot, own_peak in enumerate((peak_own, peak_other)):
        factor[slot] = jnp.exp2(own_peak[...] - peak) / total
    delta[...] = jnp.sum(weight * stats_ref[:, 2], axis=0) / total
    key_other, value_other = other_pair(place, straight, crossed)
    keys = (key_ref[:, columns(place[KV_HEAD])], key_other)
    values = (value_ref[:, columns(place[KV_HEAD])], value_other)
    for slot in range(2):
        keys_turned[slot] = keys[slot].astype(F32).T.astype(BF)
    key_total[...] = jnp.zeros_like(key_total)
    value_total[...] = jnp.zeros_like(value_total)

    def one_head(head, _):
        query = query_ref[pl.ds(place[LINE] * half, half), columns(head)]
        grad = grad_ref[:, columns(head)]
        row_delta = delta[pl.ds(head, 1), :]
        turned = jnp.zeros((HD, half), F32)
        for slot in range(2):
            expo_ref = (expo_own, expo_other)[slot]
            probs = expo_ref[head] * factor[slot, pl.ds(head, 1), :]
            score_grad = (probs * (dot(values[slot], grad, ROWS) - row_delta)).astype(BF)
            value_total[slot] += dot(probs.astype(BF), grad)
            key_total[slot] += dot(score_grad, query)
            turned += dot(keys_turned[slot], score_grad)
        result = (SCALE * turned).T.astype(BF)
        query_out[:, :, columns(head)] = result.reshape(query_out.shape[0], query_out.shape[1], HD)
        return 0

    lax.fori_loop(0, heads, one_head, 0)
    slots, chips, share, _ = keep_out.shape
    for slot in range(2):
        for chip in range(chips):
            for part, sums, scale in ((0, key_total, SCALE), (1, value_total, 1.0)):
                where = slice(part * HD, (part + 1) * HD)
                mine = pl.multiple_of((2 * chip + place[CORE]) * share, share)
                theirs = pl.multiple_of((2 * chip + 1 - place[CORE]) * share, share)
                keep_out[slot, chip, :, where] = scale * sums[slot, pl.ds(mine, share), :]
                send_out[slot, chip, :, where] = (
                    scale * sums[slot, pl.ds(theirs, share), :]
                ).astype(BF)


def on_device(
    lines,
    groups,
    parts,
    query_window,
    key_cache,
    value_cache,
    out_weight,
    grad_routed,
    token_route,
    window_start,
):
    window, local_heads = query_window.shape[0], query_window.shape[1] // HD
    half, span, rows = window // lines, key_cache.shape[0], grad_routed.shape[0]
    chips = parts // 2
    line, group, part = lax.axis_index("zh"), lax.axis_index("xy"), lax.axis_index("tp")
    chip, core = part // 2, part % 2
    kv_head = part * local_heads // GROUP
    pieces = [
        ((chip - step + chips) % chips) * 2 + (core + other) % 2
        for step in range(chips)
        for other in range(2)
    ]
    place = jnp.stack(
        [
            line,
            (line * groups + group) * span,
            ((1 - line) * groups + group) * span,
            window_start[0],
            kv_head,
            core,
        ]
        + pieces
    ).astype(jnp.int32)

    route = token_route.reshape(lines, groups, rows)
    route = jnp.where(line == 0, route, route[::-1]).transpose(1, 0, 2).reshape(1, window)
    out_weight, place, route = lax.optimization_barrier((out_weight, place, route))

    def to_pair(value):
        return lax.ppermute(value, "zh", [(0, 1), (1, 0)])

    def to_core(value):
        return lax.ppermute(value, "tp", [(i, i ^ 1) for i in range(parts)])

    def to_chip(value, step):
        return lax.ppermute(value, "tp", [(i, (i + 2 * step) % parts) for i in range(parts)])

    score_cost = pl.CostEstimate(
        flops=2 * local_heads * span * half * HD,
        bytes_accessed=4 * local_heads * span * half,
        transcendentals=local_heads * span * half,
    )
    score_outs = [
        ((local_heads, span, half), F32),
        ((local_heads, half), F32),
        ((local_heads, half), F32),
    ]
    expo_own, peak_own, total_own, weight = call(
        own_kernel,
        "own_scores",
        (place, query_window, key_cache, in_hbm(out_weight)),
        score_outs + [(out_weight.shape, BF)],
        scratch=[pltpu.SemaphoreType.DMA],
        cost=score_cost,
        streamed=(3,),
        held=(0, 3),
    )
    with jax.named_scope("gradient_rows"):
        other_rows = to_pair(grad_routed)
        other_rows, weight = lax.optimization_barrier((other_rows, weight))
        pair = jnp.stack([grad_routed, other_rows])
        chip_rows = jnp.stack([pair, to_core(pair)])
        all_rows = [chip_rows] + [to_chip(chip_rows, step) for step in range(1, chips)]
    with jax.named_scope("cache_pair"):
        mine = jnp.where(
            core == 0,
            lax.dynamic_slice_in_dim(key_cache, kv_head * HD, HD, 1),
            lax.dynamic_slice_in_dim(value_cache, kv_head * HD, HD, 1),
        )
        straight = to_pair(mine)
        crossed = to_core(straight)
    expo_other, peak_other, total_other = call(
        other_kernel,
        "other_scores",
        (place, query_window, straight, crossed),
        score_outs,
        cost=score_cost,
        held=(0,),
    )
    all_rows, straight, crossed, expo_other, peak_other, total_other = lax.optimization_barrier(
        (all_rows, straight, crossed, expo_other, peak_other, total_other)
    )
    (gathered,) = call(
        project_kernel,
        "project",
        (place, *all_rows, in_vmem(weight)),
        [((groups, lines * rows, local_heads * HD), BF)],
    )
    with jax.named_scope("head_gradients"):
        gathered = lax.all_to_all(gathered, "xy", 0, 0)
    own = (in_vmem(expo_own), peak_own)
    other = (in_vmem(expo_other), peak_other)
    grads, stats = call(
        delta_kernel,
        "deltas",
        (place, route, gathered, value_cache, straight, crossed)
        + own
        + (total_own,)
        + other
        + (total_other,),
        [((half, local_heads * HD), BF), ((groups, 3, local_heads, half), F32)],
    )
    with jax.named_scope("row_stats"):
        stats = lax.all_to_all(stats, "xy", 0, 0)
    share = span // parts
    query_part, keep, send = call(
        grads_kernel,
        "gradients",
        (place, stats, query_window, grads, key_cache, value_cache, straight, crossed) + own + other,
        [
            ((groups, half // groups, local_heads * HD), BF),
            ((2, chips, share, 2 * HD), F32),
            ((2, chips, share, 2 * HD), BF),
        ],
        scratch=[
            pltpu.VMEM((2, local_heads, half), F32),
            pltpu.VMEM((local_heads, half), F32),
            pltpu.VMEM((2, HD, span), BF),
            pltpu.VMEM((2, span, HD), F32),
            pltpu.VMEM((2, span, HD), F32),
        ],
    )
    query_terms = lax.all_to_all(query_part, "xy", 0, 0)
    with jax.named_scope("cache_terms"):
        chip_sum = keep + to_core(send).astype(F32)
        line_sum = chip_sum[0] + to_pair(chip_sum[1].astype(BF)).astype(F32)
        line_sum = line_sum.astype(BF)
        own = lax.dynamic_index_in_dim(line_sum, chip, 0, False)
        arrived = jnp.stack(
            [own]
            + [
                to_chip(lax.dynamic_index_in_dim(line_sum, (chip + step) % chips, 0, False), step)
                for step in range(1, chips)
            ]
        )
        arrived, query_terms = lax.optimization_barrier((arrived, query_terms))
        in_order = [
            lax.dynamic_index_in_dim(arrived, (chip - head + chips) % chips, 0, False)
            for head in range(chips)
        ]
        grad_keys = jnp.concatenate([piece[:, :HD] for piece in in_order], axis=1)
        grad_values = jnp.concatenate([piece[:, HD:] for piece in in_order], axis=1)
    with jax.named_scope("query_terms"):
        grad_query = jnp.sum(query_terms.astype(F32), axis=0).astype(BF)
    return grad_query, grad_keys, grad_values


def solution(mesh):
    lines = 2
    groups, parts = mesh.shape["ctx"] // lines, mesh.shape["tp"]
    fine = Mesh(mesh.devices.reshape(lines, groups, parts), ("zh", "xy", "tp"))
    ctx = ("zh", "xy")
    in_specs = (
        P(None, "tp"),
        P(ctx, None),
        P(ctx, None),
        P("tp", None),
        P(ctx, "tp"),
        P(),
        P(),
    )
    out_specs = (P(ctx, "tp"), P(ctx + ("tp",), None), P(ctx + ("tp",), None))
    return jax.shard_map(
        functools.partial(on_device, lines, groups, parts),
        mesh=fine,
        in_specs=in_specs,
        out_specs=out_specs,
        check_vma=False,
    )
```

```python
import functools
import math

import jax
import jax.numpy as jnp
from jax import lax
from jax.experimental import pallas as pl
from jax.experimental.pallas import tpu as pltpu
from jax.sharding import Mesh
from jax.sharding import PartitionSpec as P

HQ = 64
KVH = 4
HD = 128
GROUP = HQ // KVH
SCALE = 1.0 / math.sqrt(HD)
NEG = -1e30
FLOOR = -1e29
VMEM_MIB = 16
LOG2E = math.log2(math.e)

BF = jnp.bfloat16
F32 = jnp.float32
ROWS = (((1,), (1,)), ((), ()))


def dot(a, b, dims=None):
    if dims is None:
        return jnp.dot(a, b, preferred_element_type=F32)
    return lax.dot_general(a, b, dims, preferred_element_type=F32)


VMEM = pl.BlockSpec(memory_space=pltpu.VMEM)
SMEM = pl.BlockSpec(memory_space=pltpu.SMEM)


HBM = pl.BlockSpec(memory_space=pltpu.HBM)


def call(kernel, name, args, outs, scratch=(), cost=None, streamed=(), held=()):
    return pl.pallas_call(
        kernel,
        in_specs=[SMEM] + [HBM if i in streamed else VMEM for i in range(1, len(args))],
        out_specs=[VMEM] * len(outs),
        out_shape=[
            pltpu.VMEM(*out) if i in held else jax.ShapeDtypeStruct(*out)
            for i, out in enumerate(outs)
        ],
        scratch_shapes=list(scratch),
        compiler_params=pltpu.CompilerParams(vmem_limit_bytes=VMEM_MIB * 1024 * 1024),
        cost_estimate=cost,
        name=name,
    )(*args)


def in_hbm(array):
    return pltpu.with_memory_space_constraint(array, pltpu.HBM)


def in_vmem(array):
    return pltpu.with_memory_space_constraint(array, pltpu.VMEM)


LINE, FIRST, FIRST_OTHER, START, KV_HEAD, CORE, BLOCKS = range(7)


def columns(index, width=HD):
    return pl.ds(pl.multiple_of(index * width, width), width)


def project_kernel(place, *refs):
    pieces, weight_ref, out_ref = refs[:-2], refs[-2], refs[-1]
    cores, lines, rows, width = pieces[0].shape
    total = None
    for index in range(len(pieces) * cores):
        piece = pieces[index // cores][index % cores].reshape(lines * rows, width)
        term = dot(weight_ref[:, columns(place[BLOCKS + index], width)], piece, ROWS)
        total = term if total is None else total + term
    result = total.T.astype(BF)
    for copy in range(out_ref.shape[0]):
        out_ref[copy] = result


def other_pair(place, straight, crossed):
    swap = place[CORE] == 1
    first, second = straight[...], crossed[...]
    return jnp.where(swap, second, first), jnp.where(swap, first, second)


def score_heads(place, slot, first_row, query_ref, keys, expo_ref, peak_ref, total_ref):
    heads, span, window = expo_ref.shape
    query_pos = place[START] + place[LINE] * window + lax.broadcasted_iota(jnp.int32, (1, window), 1)
    key_pos = place[FIRST + slot] + lax.broadcasted_iota(jnp.int32, (span, 1), 0)

    def one_head(head, _):
        query = query_ref[pl.ds(first_row, window), columns(head)]
        scored = dot(keys, query, ROWS) * (SCALE * LOG2E)
        scored = jnp.where(key_pos <= query_pos, scored, NEG)
        peak = jnp.maximum(jnp.max(scored, axis=0, keepdims=True), FLOOR)
        expo = jnp.exp2(scored - peak)
        expo_ref[head] = expo
        peak_ref[pl.ds(head, 1), :] = peak
        total_ref[pl.ds(head, 1), :] = jnp.sum(expo, axis=0, keepdims=True)
        return 0

    lax.fori_loop(0, heads, one_head, 0)


def own_kernel(
    place,
    query_in,
    key_in,
    weight_in,
    expo_ref,
    peak_ref,
    total_ref,
    weight_out,
    query_ref,
    key_ref,
    loaded,
):
    window = query_ref.shape[0]
    rows = pl.ds(pl.multiple_of(place[LINE] * window, window), window)
    copies = [
        pltpu.make_async_copy(query_in.at[rows], query_ref, loaded.at[0]),
        pltpu.make_async_copy(key_in.at[:, columns(place[KV_HEAD])], key_ref, loaded.at[1]),
        pltpu.make_async_copy(weight_in, weight_out, loaded.at[2]),
    ]
    for copy in copies:
        copy.start()
    copies[0].wait()
    copies[1].wait()
    score_heads(place, 0, 0, query_ref, key_ref[...], expo_ref, peak_ref, total_ref)
    copies[2].wait()


def other_kernel(place, query_ref, straight, crossed, expo_ref, peak_ref, total_ref):
    keys = other_pair(place, straight, crossed)[0]
    window = expo_ref.shape[2]
    first_row = pl.multiple_of(place[LINE] * window, window)
    score_heads(place, 1, first_row, query_ref, keys, expo_ref, peak_ref, total_ref)


def delta_kernel(
    place,
    route_ref,
    gathered_ref,
    value_ref,
    straight,
    crossed,
    expo_own,
    peak_own,
    total_own,
    expo_other,
    peak_other,
    total_other,
    grad_ref,
    stats_ref,
):
    heads, span, half = expo_own.shape
    window = route_ref.shape[1]
    token = place[LINE] * half + lax.broadcasted_iota(jnp.int32, (half, window), 0)
    pick = jnp.where(route_ref[...] == token, 1.0, 0.0).astype(BF)
    values = (value_ref[:, columns(place[KV_HEAD])], other_pair(place, straight, crossed)[1])
    grad_ref[...] = dot(pick, gathered_ref[...].reshape(window, heads * HD)).astype(BF)
    peak = jnp.maximum(peak_own[...], peak_other[...])
    factors = (jnp.exp2(peak_own[...] - peak), jnp.exp2(peak_other[...] - peak))
    stats_ref[0, 0] = peak
    stats_ref[0, 1] = total_own[...] * factors[0] + total_other[...] * factors[1]

    def one_head(head, _):
        grad = grad_ref[:, columns(head)]
        for slot, expo_ref in enumerate((expo_own, expo_other)):
            stats_ref[1 + slot, 2, pl.ds(head, 1), :] = jnp.sum(
                expo_ref[head] * dot(values[slot], grad, ROWS), axis=0, keepdims=True
            )
        return 0

    lax.fori_loop(0, heads, one_head, 0)
    stats_ref[0, 2] = stats_ref[1, 2] * factors[0] + stats_ref[2, 2] * factors[1]
    for copy in range(1, stats_ref.shape[0]):
        stats_ref[copy] = stats_ref[0]


def grads_kernel(
    place,
    stats_ref,
    query_ref,
    grad_ref,
    key_ref,
    value_ref,
    straight,
    crossed,
    expo_own,
    peak_own,
    expo_other,
    peak_other,
    query_out,
    keep_out,
    send_out,
    factor,
    delta,
    keys_turned,
    key_total,
    value_total,
):
    heads, span, half = expo_own.shape
    peaks = stats_ref[:, 0]
    peak = jnp.max(peaks, axis=0)
    weight = jnp.exp2(peaks - peak[None])
    total = jnp.sum(weight * stats_ref[:, 1], axis=0)
    for slot, own_peak in enumerate((peak_own, peak_other)):
        factor[slot] = jnp.exp2(own_peak[...] - peak) / total
    delta[...] = jnp.sum(weight * stats_ref[:, 2], axis=0) / total
    key_other, value_other = other_pair(place, straight, crossed)
    keys = (key_ref[:, columns(place[KV_HEAD])], key_other)
    values = (value_ref[:, columns(place[KV_HEAD])], value_other)
    for slot in range(2):
        keys_turned[slot] = keys[slot].astype(F32).T.astype(BF)
    key_total[...] = jnp.zeros_like(key_total)
    value_total[...] = jnp.zeros_like(value_total)

    def one_head(head, _):
        query = query_ref[pl.ds(place[LINE] * half, half), columns(head)]
        grad = grad_ref[:, columns(head)]
        row_delta = delta[pl.ds(head, 1), :]
        turned = jnp.zeros((HD, half), F32)
        for slot in range(2):
            expo_ref = (expo_own, expo_other)[slot]
            probs = expo_ref[head] * factor[slot, pl.ds(head, 1), :]
            score_grad = (probs * (dot(values[slot], grad, ROWS) - row_delta)).astype(BF)
            value_total[slot] += dot(probs.astype(BF), grad)
            key_total[slot] += dot(score_grad, query)
            turned += dot(keys_turned[slot], score_grad)
        result = (SCALE * turned).T.astype(BF)
        query_out[:, :, columns(head)] = result.reshape(query_out.shape[0], query_out.shape[1], HD)
        return 0

    lax.fori_loop(0, heads, one_head, 0)
    slots, chips, share, _ = keep_out.shape
    for slot in range(2):
        for chip in range(chips):
            for part, sums, scale in ((0, key_total, SCALE), (1, value_total, 1.0)):
                where = slice(part * HD, (part + 1) * HD)
                mine = pl.multiple_of((2 * chip + place[CORE]) * share, share)
                theirs = pl.multiple_of((2 * chip + 1 - place[CORE]) * share, share)
                keep_out[slot, chip, :, where] = scale * sums[slot, pl.ds(mine, share), :]
                send_out[slot, chip, :, where] = (
                    scale * sums[slot, pl.ds(theirs, share), :]
                ).astype(BF)


def finish_kernel(place, terms_ref, *refs):
    pieces, (query_out, key_out, value_out) = refs[:-3], refs[-3:]
    query_out[...] = jnp.sum(terms_ref[...].astype(F32), axis=0).astype(BF)
    for step, piece in enumerate(pieces):
        where = columns(place[BLOCKS + 2 * step] // 2)
        key_out[:, where] = piece[:, :HD]
        value_out[:, where] = piece[:, HD:]


def on_device(
    lines,
    groups,
    parts,
    query_window,
    key_cache,
    value_cache,
    out_weight,
    grad_routed,
    token_route,
    window_start,
):
    window, local_heads = query_window.shape[0], query_window.shape[1] // HD
    half, span, rows = window // lines, key_cache.shape[0], grad_routed.shape[0]
    chips = parts // 2
    line, group, part = lax.axis_index("zh"), lax.axis_index("xy"), lax.axis_index("tp")
    chip, core = part // 2, part % 2
    kv_head = part * local_heads // GROUP
    pieces = [
        ((chip - step + chips) % chips) * 2 + (core + other) % 2
        for step in range(chips)
        for other in range(2)
    ]
    place = jnp.stack(
        [
            line,
            (line * groups + group) * span,
            ((1 - line) * groups + group) * span,
            window_start[0],
            kv_head,
            core,
        ]
        + pieces
    ).astype(jnp.int32)

    route = token_route.reshape(lines, groups, rows)
    route = jnp.where(line == 0, route, route[::-1]).transpose(1, 0, 2).reshape(1, window)
    def to_pair(value):
        return lax.ppermute(value, "zh", [(0, 1), (1, 0)])

    def to_core(value):
        return lax.ppermute(value, "tp", [(i, i ^ 1) for i in range(parts)])

    def to_chip(value, step):
        return lax.ppermute(value, "tp", [(i, (i + 2 * step) % parts) for i in range(parts)])

    score_cost = pl.CostEstimate(
        flops=2 * local_heads * span * half * HD,
        bytes_accessed=4 * local_heads * span * half,
        transcendentals=local_heads * span * half,
    )
    score_outs = [
        ((local_heads, span, half), F32),
        ((local_heads, half), F32),
        ((local_heads, half), F32),
    ]
    expo_own, peak_own, total_own, weight = call(
        own_kernel,
        "own_scores",
        (place, in_hbm(query_window), in_hbm(key_cache), in_hbm(out_weight)),
        score_outs + [(out_weight.shape, BF)],
        scratch=[
            pltpu.VMEM((half, local_heads * HD), BF),
            pltpu.VMEM((span, HD), BF),
            pltpu.SemaphoreType.DMA((3,)),
        ],
        cost=score_cost,
        streamed=(1, 2, 3),
        held=(0, 3),
    )
    with jax.named_scope("gradient_rows"):
        other_rows = to_pair(grad_routed)
        other_rows, weight, route = lax.optimization_barrier((other_rows, weight, route))
        pair = jnp.stack([grad_routed, other_rows])
        chip_rows = jnp.stack([pair, to_core(pair)])
        all_rows = [chip_rows] + [to_chip(chip_rows, step) for step in range(1, chips)]
    with jax.named_scope("cache_pair"):
        mine = jnp.where(
            core == 0,
            lax.dynamic_slice_in_dim(key_cache, kv_head * HD, HD, 1),
            lax.dynamic_slice_in_dim(value_cache, kv_head * HD, HD, 1),
        )
        straight = to_pair(mine)
        crossed = to_core(straight)
    expo_other, peak_other, total_other = call(
        other_kernel,
        "other_scores",
        (place, query_window, straight, crossed),
        score_outs,
        cost=score_cost,
        held=(0,),
    )
    all_rows, straight, crossed, expo_other, peak_other, total_other = lax.optimization_barrier(
        (all_rows, straight, crossed, expo_other, peak_other, total_other)
    )
    (gathered,) = call(
        project_kernel,
        "project",
        (place, *all_rows, in_vmem(weight)),
        [((groups, lines * rows, local_heads * HD), BF)],
    )
    with jax.named_scope("head_gradients"):
        gathered = lax.all_to_all(gathered, "xy", 0, 0)
    own = (in_vmem(expo_own), peak_own)
    other = (in_vmem(expo_other), peak_other)
    grads, stats = call(
        delta_kernel,
        "deltas",
        (place, route, gathered, value_cache, straight, crossed)
        + own
        + (total_own,)
        + other
        + (total_other,),
        [((half, local_heads * HD), BF), ((groups, 3, local_heads, half), F32)],
    )
    with jax.named_scope("row_stats"):
        stats = lax.all_to_all(stats, "xy", 0, 0)
    share = span // parts
    query_part, keep, send = call(
        grads_kernel,
        "gradients",
        (place, stats, query_window, grads, key_cache, value_cache, straight, crossed) + own + other,
        [
            ((groups, half // groups, local_heads * HD), BF),
            ((2, chips, share, 2 * HD), F32),
            ((2, chips, share, 2 * HD), BF),
        ],
        scratch=[
            pltpu.VMEM((2, local_heads, half), F32),
            pltpu.VMEM((local_heads, half), F32),
            pltpu.VMEM((2, HD, span), BF),
            pltpu.VMEM((2, span, HD), F32),
            pltpu.VMEM((2, span, HD), F32),
        ],
    )
    query_terms = lax.all_to_all(query_part, "xy", 0, 0)
    with jax.named_scope("cache_terms"):
        chip_sum = keep + to_core(send).astype(F32)
        line_sum = chip_sum[0] + to_pair(chip_sum[1].astype(BF)).astype(F32)
        line_sum = line_sum.astype(BF)
        own = lax.dynamic_index_in_dim(line_sum, chip, 0, False)
        arrived = [own] + [
            to_chip(lax.dynamic_index_in_dim(line_sum, (chip + step) % chips, 0, False), step)
            for step in range(1, chips)
        ]
    query_terms, *arrived = lax.optimization_barrier((query_terms, *arrived))
    width = KVH * HD
    return call(
        finish_kernel,
        "finish",
        (place, query_terms, *arrived),
        [
            (query_terms.shape[1:], BF),
            ((share, width), BF),
            ((share, width), BF),
        ],
    )


def solution(mesh):
    lines = 2
    groups, parts = mesh.shape["ctx"] // lines, mesh.shape["tp"]
    fine = Mesh(mesh.devices.reshape(lines, groups, parts), ("zh", "xy", "tp"))
    ctx = ("zh", "xy")
    in_specs = (
        P(None, "tp"),
        P(ctx, None),
        P(ctx, None),
        P("tp", None),
        P(ctx, "tp"),
        P(),
        P(),
    )
    out_specs = (P(ctx, "tp"), P(ctx + ("tp",), None), P(ctx + ("tp",), None))
    return jax.shard_map(
        functools.partial(on_device, lines, groups, parts),
        mesh=fine,
        in_specs=in_specs,
        out_specs=out_specs,
        check_vma=False,
    )
```

```python
import functools
import math

import jax
import jax.numpy as jnp
from jax import lax
from jax.experimental import pallas as pl
from jax.experimental.pallas import tpu as pltpu
from jax.sharding import Mesh
from jax.sharding import PartitionSpec as P

HQ = 64
KVH = 4
HD = 128
GROUP = HQ // KVH
SCALE = 1.0 / math.sqrt(HD)
NEG = -1e30
FLOOR = -1e29
VMEM_MIB = 16
LOG2E = math.log2(math.e)

BF = jnp.bfloat16
F32 = jnp.float32
ROWS = (((1,), (1,)), ((), ()))


def dot(a, b, dims=None):
    if dims is None:
        return jnp.dot(a, b, preferred_element_type=F32)
    return lax.dot_general(a, b, dims, preferred_element_type=F32)


VMEM = pl.BlockSpec(memory_space=pltpu.VMEM)
SMEM = pl.BlockSpec(memory_space=pltpu.SMEM)


HBM = pl.BlockSpec(memory_space=pltpu.HBM)


def call(kernel, name, args, outs, scratch=(), cost=None, streamed=(), held=()):
    return pl.pallas_call(
        kernel,
        in_specs=[SMEM] + [HBM if i in streamed else VMEM for i in range(1, len(args))],
        out_specs=[VMEM] * len(outs),
        out_shape=[
            pltpu.VMEM(*out) if i in held else jax.ShapeDtypeStruct(*out)
            for i, out in enumerate(outs)
        ],
        scratch_shapes=list(scratch),
        compiler_params=pltpu.CompilerParams(vmem_limit_bytes=VMEM_MIB * 1024 * 1024),
        cost_estimate=cost,
        name=name,
    )(*args)


def in_hbm(array):
    return pltpu.with_memory_space_constraint(array, pltpu.HBM)


def in_vmem(array):
    return pltpu.with_memory_space_constraint(array, pltpu.VMEM)


LINE, FIRST, FIRST_OTHER, START, KV_HEAD, CORE, BLOCKS = range(7)


def columns(index, width=HD):
    return pl.ds(pl.multiple_of(index * width, width), width)


def project_kernel(place, *refs):
    pieces, weight_ref, out_ref = refs[:-2], refs[-2], refs[-1]
    cores, lines, rows, width = pieces[0].shape
    total = None
    for index in range(len(pieces) * cores):
        piece = pieces[index // cores][index % cores].reshape(lines * rows, width)
        term = dot(weight_ref[:, columns(place[BLOCKS + index], width)], piece, ROWS)
        total = term if total is None else total + term
    result = total.T.astype(BF)
    for copy in range(out_ref.shape[0]):
        out_ref[copy] = result


def other_pair(place, straight, crossed):
    swap = place[CORE] == 1
    first, second = straight[...], crossed[...]
    return jnp.where(swap, second, first), jnp.where(swap, first, second)


def score_heads(place, slot, first_row, query_ref, keys, expo_ref, peak_ref, total_ref):
    heads, span, window = expo_ref.shape
    query_pos = place[START] + place[LINE] * window + lax.broadcasted_iota(jnp.int32, (1, window), 1)
    key_pos = place[FIRST + slot] + lax.broadcasted_iota(jnp.int32, (span, 1), 0)

    def one_head(head, _):
        query = query_ref[pl.ds(first_row, window), columns(head)]
        scored = dot(keys, query, ROWS) * (SCALE * LOG2E)
        scored = jnp.where(key_pos <= query_pos, scored, NEG)
        peak = jnp.maximum(jnp.max(scored, axis=0, keepdims=True), FLOOR)
        expo = jnp.exp2(scored - peak)
        expo_ref[head] = expo
        peak_ref[pl.ds(head, 1), :] = peak
        total_ref[pl.ds(head, 1), :] = jnp.sum(expo, axis=0, keepdims=True)
        return 0

    lax.fori_loop(0, heads, one_head, 0, unroll=True)


def own_kernel(
    place,
    query_in,
    key_in,
    weight_in,
    expo_ref,
    peak_ref,
    total_ref,
    weight_out,
    query_ref,
    key_ref,
    loaded,
):
    window = query_ref.shape[0]
    rows = pl.ds(pl.multiple_of(place[LINE] * window, window), window)
    copies = [
        pltpu.make_async_copy(query_in.at[rows], query_ref, loaded.at[0]),
        pltpu.make_async_copy(key_in.at[:, columns(place[KV_HEAD])], key_ref, loaded.at[1]),
        pltpu.make_async_copy(weight_in, weight_out, loaded.at[2]),
    ]
    for copy in copies:
        copy.start()
    copies[0].wait()
    copies[1].wait()
    score_heads(place, 0, 0, query_ref, key_ref[...], expo_ref, peak_ref, total_ref)
    copies[2].wait()


def other_kernel(place, query_ref, straight, crossed, expo_ref, peak_ref, total_ref):
    keys = other_pair(place, straight, crossed)[0]
    window = expo_ref.shape[2]
    first_row = pl.multiple_of(place[LINE] * window, window)
    score_heads(place, 1, first_row, query_ref, keys, expo_ref, peak_ref, total_ref)


def delta_kernel(
    place,
    route_ref,
    gathered_ref,
    value_ref,
    straight,
    crossed,
    expo_own,
    peak_own,
    total_own,
    expo_other,
    peak_other,
    total_other,
    grad_ref,
    stats_ref,
    probs_grad_ref,
):
    heads, span, half = expo_own.shape
    window = route_ref.shape[1]
    token = place[LINE] * half + lax.broadcasted_iota(jnp.int32, (half, window), 0)
    pick = jnp.where(route_ref[...] == token, 1.0, 0.0).astype(BF)
    values = (value_ref[:, columns(place[KV_HEAD])], other_pair(place, straight, crossed)[1])
    grad_ref[...] = dot(pick, gathered_ref[...].reshape(window, heads * HD)).astype(BF)
    peak = jnp.maximum(peak_own[...], peak_other[...])
    factors = (jnp.exp2(peak_own[...] - peak), jnp.exp2(peak_other[...] - peak))
    stats_ref[0, 0] = peak
    stats_ref[0, 1] = total_own[...] * factors[0] + total_other[...] * factors[1]

    def one_head(head, _):
        grad = grad_ref[:, columns(head)]
        for slot, expo_ref in enumerate((expo_own, expo_other)):
            grad_probs = dot(values[slot], grad, ROWS)
            probs_grad_ref[head, slot] = grad_probs
            stats_ref[1 + slot, 2, pl.ds(head, 1), :] = jnp.sum(
                expo_ref[head] * grad_probs, axis=0, keepdims=True
            )
        return 0

    lax.fori_loop(0, heads, one_head, 0, unroll=True)
    stats_ref[0, 2] = stats_ref[1, 2] * factors[0] + stats_ref[2, 2] * factors[1]
    for copy in range(1, stats_ref.shape[0]):
        stats_ref[copy] = stats_ref[0]


def grads_kernel(
    place,
    stats_ref,
    query_ref,
    grad_ref,
    key_ref,
    straight,
    crossed,
    probs_grad_ref,
    expo_own,
    peak_own,
    expo_other,
    peak_other,
    query_out,
    keep_out,
    send_out,
    factor,
    delta,
    keys_turned,
    key_total,
    value_total,
):
    heads, span, half = expo_own.shape
    peaks = stats_ref[:, 0]
    peak = jnp.max(peaks, axis=0)
    weight = jnp.exp2(peaks - peak[None])
    total = jnp.sum(weight * stats_ref[:, 1], axis=0)
    for slot, own_peak in enumerate((peak_own, peak_other)):
        factor[slot] = jnp.exp2(own_peak[...] - peak) / total
    delta[...] = jnp.sum(weight * stats_ref[:, 2], axis=0) / total
    keys = (key_ref[:, columns(place[KV_HEAD])], other_pair(place, straight, crossed)[0])
    for slot in range(2):
        keys_turned[slot] = keys[slot].astype(F32).T.astype(BF)
    key_total[...] = jnp.zeros_like(key_total)
    value_total[...] = jnp.zeros_like(value_total)

    def one_head(head, _):
        query = query_ref[pl.ds(place[LINE] * half, half), columns(head)]
        grad = grad_ref[:, columns(head)]
        row_delta = delta[pl.ds(head, 1), :]
        turned = jnp.zeros((HD, half), F32)
        for slot in range(2):
            expo_ref = (expo_own, expo_other)[slot]
            probs = expo_ref[head] * factor[slot, pl.ds(head, 1), :]
            score_grad = (probs * (probs_grad_ref[head, slot] - row_delta)).astype(BF)
            value_total[slot] += dot(probs.astype(BF), grad)
            key_total[slot] += dot(score_grad, query)
            turned += dot(keys_turned[slot], score_grad)
        result = (SCALE * turned).T.astype(BF)
        query_out[:, :, columns(head)] = result.reshape(query_out.shape[0], query_out.shape[1], HD)
        return 0

    lax.fori_loop(0, heads, one_head, 0, unroll=True)
    slots, chips, share, _ = keep_out.shape
    for slot in range(2):
        for chip in range(chips):
            for part, sums, scale in ((0, key_total, SCALE), (1, value_total, 1.0)):
                where = slice(part * HD, (part + 1) * HD)
                mine = pl.multiple_of((2 * chip + place[CORE]) * share, share)
                theirs = pl.multiple_of((2 * chip + 1 - place[CORE]) * share, share)
                keep_out[slot, chip, :, where] = scale * sums[slot, pl.ds(mine, share), :]
                send_out[slot, chip, :, where] = (
                    scale * sums[slot, pl.ds(theirs, share), :]
                ).astype(BF)


def finish_kernel(place, terms_ref, *refs):
    pieces, (query_out, key_out, value_out) = refs[:-3], refs[-3:]
    query_out[...] = jnp.sum(terms_ref[...].astype(F32), axis=0).astype(BF)
    for step, piece in enumerate(pieces):
        where = columns(place[BLOCKS + 2 * step] // 2)
        key_out[:, where] = piece[:, :HD]
        value_out[:, where] = piece[:, HD:]


def on_device(
    lines,
    groups,
    parts,
    query_window,
    key_cache,
    value_cache,
    out_weight,
    grad_routed,
    token_route,
    window_start,
):
    window, local_heads = query_window.shape[0], query_window.shape[1] // HD
    half, span, rows = window // lines, key_cache.shape[0], grad_routed.shape[0]
    chips = parts // 2
    line, group, part = lax.axis_index("zh"), lax.axis_index("xy"), lax.axis_index("tp")
    chip, core = part // 2, part % 2
    kv_head = part * local_heads // GROUP
    pieces = [
        ((chip - step + chips) % chips) * 2 + (core + other) % 2
        for step in range(chips)
        for other in range(2)
    ]
    place = jnp.stack(
        [
            line,
            (line * groups + group) * span,
            ((1 - line) * groups + group) * span,
            window_start[0],
            kv_head,
            core,
        ]
        + pieces
    ).astype(jnp.int32)

    route = token_route.reshape(lines, groups, rows)
    route = jnp.where(line == 0, route, route[::-1]).transpose(1, 0, 2).reshape(1, window)
    def to_pair(value):
        return lax.ppermute(value, "zh", [(0, 1), (1, 0)])

    def to_core(value):
        return lax.ppermute(value, "tp", [(i, i ^ 1) for i in range(parts)])

    def to_chip(value, step):
        return lax.ppermute(value, "tp", [(i, (i + 2 * step) % parts) for i in range(parts)])

    score_cost = pl.CostEstimate(
        flops=2 * local_heads * span * half * HD,
        bytes_accessed=4 * local_heads * span * half,
        transcendentals=local_heads * span * half,
    )
    score_outs = [
        ((local_heads, span, half), F32),
        ((local_heads, half), F32),
        ((local_heads, half), F32),
    ]
    expo_own, peak_own, total_own, weight = call(
        own_kernel,
        "own_scores",
        (place, in_hbm(query_window), in_hbm(key_cache), in_hbm(out_weight)),
        score_outs + [(out_weight.shape, BF)],
        scratch=[
            pltpu.VMEM((half, local_heads * HD), BF),
            pltpu.VMEM((span, HD), BF),
            pltpu.SemaphoreType.DMA((3,)),
        ],
        cost=score_cost,
        streamed=(1, 2, 3),
        held=(0, 3),
    )
    with jax.named_scope("gradient_rows"):
        other_rows = to_pair(grad_routed)
        other_rows, weight, route = lax.optimization_barrier((other_rows, weight, route))
        pair = jnp.stack([grad_routed, other_rows])
        chip_rows = jnp.stack([pair, to_core(pair)])
        all_rows = [chip_rows] + [to_chip(chip_rows, step) for step in range(1, chips)]
    with jax.named_scope("cache_pair"):
        mine = jnp.where(
            core == 0,
            lax.dynamic_slice_in_dim(key_cache, kv_head * HD, HD, 1),
            lax.dynamic_slice_in_dim(value_cache, kv_head * HD, HD, 1),
        )
        straight = to_pair(mine)
        crossed = to_core(straight)
    expo_other, peak_other, total_other = call(
        other_kernel,
        "other_scores",
        (place, query_window, straight, crossed),
        score_outs,
        cost=score_cost,
        held=(0,),
    )
    all_rows, straight, crossed, expo_other, peak_other, total_other = lax.optimization_barrier(
        (all_rows, straight, crossed, expo_other, peak_other, total_other)
    )
    (gathered,) = call(
        project_kernel,
        "project",
        (place, *all_rows, in_vmem(weight)),
        [((groups, lines * rows, local_heads * HD), BF)],
    )
    with jax.named_scope("head_gradients"):
        gathered = lax.all_to_all(gathered, "xy", 0, 0)
    own = (in_vmem(expo_own), peak_own)
    other = (in_vmem(expo_other), peak_other)
    grads, stats, probs_grad = call(
        delta_kernel,
        "deltas",
        (place, route, gathered, value_cache, straight, crossed)
        + own
        + (total_own,)
        + other
        + (total_other,),
        [
            ((half, local_heads * HD), BF),
            ((groups, 3, local_heads, half), F32),
            ((local_heads, 2, span, half), F32),
        ],
        held=(2,),
    )
    with jax.named_scope("row_stats"):
        stats = lax.all_to_all(stats, "xy", 0, 0)
    share = span // parts
    query_part, keep, send = call(
        grads_kernel,
        "gradients",
        (place, stats, query_window, grads, key_cache, straight, crossed, in_vmem(probs_grad)) + own + other,
        [
            ((groups, half // groups, local_heads * HD), BF),
            ((2, chips, share, 2 * HD), F32),
            ((2, chips, share, 2 * HD), BF),
        ],
        scratch=[
            pltpu.VMEM((2, local_heads, half), F32),
            pltpu.VMEM((local_heads, half), F32),
            pltpu.VMEM((2, HD, span), BF),
            pltpu.VMEM((2, span, HD), F32),
            pltpu.VMEM((2, span, HD), F32),
        ],
    )
    query_terms = lax.all_to_all(query_part, "xy", 0, 0)
    with jax.named_scope("cache_terms"):
        chip_sum = keep + to_core(send).astype(F32)
        line_sum = chip_sum[0] + to_pair(chip_sum[1].astype(BF)).astype(F32)
        line_sum = line_sum.astype(BF)
        own = lax.dynamic_index_in_dim(line_sum, chip, 0, False)
        arrived = [own] + [
            to_chip(lax.dynamic_index_in_dim(line_sum, (chip + step) % chips, 0, False), step)
            for step in range(1, chips)
        ]
    query_terms, *arrived = lax.optimization_barrier((query_terms, *arrived))
    width = KVH * HD
    return call(
        finish_kernel,
        "finish",
        (place, query_terms, *arrived),
        [
            (query_terms.shape[1:], BF),
            ((share, width), BF),
            ((share, width), BF),
        ],
    )


def solution(mesh):
    lines = 2
    groups, parts = mesh.shape["ctx"] // lines, mesh.shape["tp"]
    fine = Mesh(mesh.devices.reshape(lines, groups, parts), ("zh", "xy", "tp"))
    ctx = ("zh", "xy")
    in_specs = (
        P(None, "tp"),
        P(ctx, None),
        P(ctx, None),
        P("tp", None),
        P(ctx, "tp"),
        P(),
        P(),
    )
    out_specs = (P(ctx, "tp"), P(ctx + ("tp",), None), P(ctx + ("tp",), None))
    return jax.shard_map(
        functools.partial(on_device, lines, groups, parts),
        mesh=fine,
        in_specs=in_specs,
        out_specs=out_specs,
        check_vma=False,
    )
```

```python
import functools
import math

import jax
import jax.numpy as jnp
from jax import lax
from jax.experimental import pallas as pl
from jax.experimental.pallas import tpu as pltpu
from jax.sharding import Mesh
from jax.sharding import PartitionSpec as P

HQ = 64
KVH = 4
HD = 128
GROUP = HQ // KVH
SCALE = 1.0 / math.sqrt(HD)
NEG = -1e30
FLOOR = -1e29
VMEM_MIB = 16
LOG2E = math.log2(math.e)

BF = jnp.bfloat16
F32 = jnp.float32
ROWS = (((1,), (1,)), ((), ()))


def dot(a, b, dims=None):
    if dims is None:
        return jnp.dot(a, b, preferred_element_type=F32)
    return lax.dot_general(a, b, dims, preferred_element_type=F32)


VMEM = pl.BlockSpec(memory_space=pltpu.VMEM)
SMEM = pl.BlockSpec(memory_space=pltpu.SMEM)


HBM = pl.BlockSpec(memory_space=pltpu.HBM)


def call(kernel, name, args, outs, scratch=(), cost=None, streamed=(), held=()):
    return pl.pallas_call(
        kernel,
        in_specs=[SMEM] + [HBM if i in streamed else VMEM for i in range(1, len(args))],
        out_specs=[VMEM] * len(outs),
        out_shape=[
            pltpu.VMEM(*out) if i in held else jax.ShapeDtypeStruct(*out)
            for i, out in enumerate(outs)
        ],
        scratch_shapes=list(scratch),
        compiler_params=pltpu.CompilerParams(vmem_limit_bytes=VMEM_MIB * 1024 * 1024),
        cost_estimate=cost,
        name=name,
    )(*args)


def in_hbm(array):
    return pltpu.with_memory_space_constraint(array, pltpu.HBM)


def in_vmem(array):
    return pltpu.with_memory_space_constraint(array, pltpu.VMEM)


LINE, FIRST, FIRST_OTHER, START, KV_HEAD, CORE, BLOCKS = range(7)


def columns(index, width=HD):
    return pl.ds(pl.multiple_of(index * width, width), width)


def project_kernel(place, *refs):
    pieces, weight_ref, out_ref = refs[:-2], refs[-2], refs[-1]
    cores, _, width = pieces[0].shape
    total = None
    for index in range(len(pieces) * cores):
        piece = pieces[index // cores][index % cores]
        term = dot(weight_ref[:, columns(place[BLOCKS + index], width)], piece, ROWS)
        total = term if total is None else total + term
    result = total.T.astype(BF)
    for copy in range(out_ref.shape[0]):
        out_ref[copy] = result


def other_pair(place, straight, crossed):
    swap = place[CORE] == 1
    first, second = straight[...], crossed[...]
    return jnp.where(swap, second, first), jnp.where(swap, first, second)


def picked(place, route_ref, window, half):
    tokens = route_ref[:, columns(place[LINE], half)]
    rows = lax.broadcasted_iota(jnp.int32, (window, half), 0) == tokens
    return tokens, jnp.where(rows, 1.0, 0.0).astype(BF)


def score_heads(place, slot, query_pos, query_ref, keys, expo_ref, peak_ref, total_ref):
    heads, span, _ = expo_ref.shape
    key_pos = place[FIRST + slot] + lax.broadcasted_iota(jnp.int32, (span, 1), 0)

    def one_head(head, _):
        scored = dot(keys, query_ref[:, columns(head)], ROWS) * (SCALE * LOG2E)
        scored = jnp.where(key_pos <= query_pos, scored, NEG)
        peak = jnp.maximum(jnp.max(scored, axis=0, keepdims=True), FLOOR)
        expo = jnp.exp2(scored - peak)
        expo_ref[head] = expo
        peak_ref[pl.ds(head, 1), :] = peak
        total_ref[pl.ds(head, 1), :] = jnp.sum(expo, axis=0, keepdims=True)
        return 0

    lax.fori_loop(0, heads, one_head, 0, unroll=True)


def own_kernel(
    place,
    route_ref,
    query_in,
    key_in,
    weight_in,
    expo_ref,
    peak_ref,
    total_ref,
    weight_out,
    query_ref,
    all_query_ref,
    key_ref,
    loaded,
):
    copies = [
        pltpu.make_async_copy(query_in, all_query_ref, loaded.at[0]),
        pltpu.make_async_copy(key_in.at[:, columns(place[KV_HEAD])], key_ref, loaded.at[1]),
        pltpu.make_async_copy(weight_in, weight_out, loaded.at[2]),
    ]
    for copy in copies:
        copy.start()
    tokens, pick = picked(place, route_ref, all_query_ref.shape[0], query_ref.shape[0])
    copies[0].wait()
    copies[1].wait()
    query_ref[...] = dot(pick, all_query_ref[...], (((0,), (0,)), ((), ()))).astype(BF)
    score_heads(
        place, 0, place[START] + tokens, query_ref, key_ref[...], expo_ref, peak_ref, total_ref
    )
    copies[2].wait()


def other_kernel(place, route_ref, query_ref, straight, crossed, expo_ref, peak_ref, total_ref):
    keys = other_pair(place, straight, crossed)[0]
    query_pos = place[START] + route_ref[:, columns(place[LINE], expo_ref.shape[2])]
    score_heads(place, 1, query_pos, query_ref, keys, expo_ref, peak_ref, total_ref)


def delta_kernel(
    place,
    grad_ref,
    value_ref,
    straight,
    crossed,
    expo_own,
    peak_own,
    total_own,
    expo_other,
    peak_other,
    total_other,
    stats_ref,
    probs_grad_ref,
):
    heads, span, half = expo_own.shape
    values = (value_ref[:, columns(place[KV_HEAD])], other_pair(place, straight, crossed)[1])
    peak = jnp.maximum(peak_own[...], peak_other[...])
    factors = (jnp.exp2(peak_own[...] - peak), jnp.exp2(peak_other[...] - peak))
    stats_ref[0, 0] = peak
    stats_ref[0, 1] = total_own[...] * factors[0] + total_other[...] * factors[1]

    def one_head(head, _):
        grad = grad_ref[:, columns(head)]
        for slot, expo_ref in enumerate((expo_own, expo_other)):
            grad_probs = dot(values[slot], grad, ROWS)
            probs_grad_ref[head, slot] = grad_probs
            stats_ref[1 + slot, 2, pl.ds(head, 1), :] = jnp.sum(
                expo_ref[head] * grad_probs, axis=0, keepdims=True
            )
        return 0

    lax.fori_loop(0, heads, one_head, 0, unroll=True)
    stats_ref[0, 2] = stats_ref[1, 2] * factors[0] + stats_ref[2, 2] * factors[1]
    for copy in range(1, stats_ref.shape[0]):
        stats_ref[copy] = stats_ref[0]


def grads_kernel(
    place,
    route_ref,
    stats_ref,
    query_ref,
    grad_ref,
    key_ref,
    straight,
    crossed,
    probs_grad_ref,
    expo_own,
    peak_own,
    expo_other,
    peak_other,
    query_out,
    keep_out,
    send_out,
    factor,
    delta,
    keys_turned,
    key_total,
    value_total,
):
    heads, span, half = expo_own.shape
    owners, rows, _ = query_out.shape
    rows //= 2
    _, pick = picked(place, route_ref, 2 * half, half)
    peaks = stats_ref[:, 0]
    peak = jnp.max(peaks, axis=0)
    weight = jnp.exp2(peaks - peak[None])
    total = jnp.sum(weight * stats_ref[:, 1], axis=0)
    for slot, own_peak in enumerate((peak_own, peak_other)):
        factor[slot] = jnp.exp2(own_peak[...] - peak) / total
    delta[...] = jnp.sum(weight * stats_ref[:, 2], axis=0) / total
    keys = (key_ref[:, columns(place[KV_HEAD])], other_pair(place, straight, crossed)[0])
    for slot in range(2):
        keys_turned[slot] = keys[slot].astype(F32).T.astype(BF)
    key_total[...] = jnp.zeros_like(key_total)
    value_total[...] = jnp.zeros_like(value_total)

    def one_head(head, _):
        query = query_ref[:, columns(head)]
        grad = grad_ref[:, columns(head)]
        row_delta = delta[pl.ds(head, 1), :]
        turned = jnp.zeros((HD, half), F32)
        for slot in range(2):
            expo_ref = (expo_own, expo_other)[slot]
            probs = expo_ref[head] * factor[slot, pl.ds(head, 1), :]
            score_grad = (probs * (probs_grad_ref[head, slot] - row_delta)).astype(BF)
            value_total[slot] += dot(probs.astype(BF), grad)
            key_total[slot] += dot(score_grad, query)
            turned += dot(keys_turned[slot], score_grad)
        result = dot(pick, (SCALE * turned).astype(BF), ROWS).astype(BF)
        for line in range(2):
            query_out[:, line * rows : (line + 1) * rows, columns(head)] = result[
                line * half : (line + 1) * half
            ].reshape(owners, rows, HD)
        return 0

    lax.fori_loop(0, heads, one_head, 0, unroll=True)
    slots, chips, share, _ = keep_out.shape
    for slot in range(2):
        for chip in range(chips):
            for part, sums, scale in ((0, key_total, SCALE), (1, value_total, 1.0)):
                where = slice(part * HD, (part + 1) * HD)
                mine = pl.multiple_of((2 * chip + place[CORE]) * share, share)
                theirs = pl.multiple_of((2 * chip + 1 - place[CORE]) * share, share)
                keep_out[slot, chip, :, where] = scale * sums[slot, pl.ds(mine, share), :]
                send_out[slot, chip, :, where] = (
                    scale * sums[slot, pl.ds(theirs, share), :]
                ).astype(BF)


def query_kernel(place, terms_ref, keep_ref, send_ref):
    rows = keep_ref.shape[0]
    mine = pl.multiple_of(place[LINE] * rows, rows)
    theirs = pl.multiple_of((1 - place[LINE]) * rows, rows)
    keep_ref[...] = jnp.sum(terms_ref[:, pl.ds(mine, rows)].astype(F32), axis=0)
    send_ref[...] = jnp.sum(terms_ref[:, pl.ds(theirs, rows)].astype(F32), axis=0).astype(BF)


def finish_kernel(place, kept_ref, came_ref, *refs):
    pieces, (query_out, key_out, value_out) = refs[:-3], refs[-3:]
    query_out[...] = (kept_ref[...] + came_ref[...].astype(F32)).astype(BF)
    for step, piece in enumerate(pieces):
        where = columns(place[BLOCKS + 2 * step] // 2)
        key_out[:, where] = piece[:, :HD]
        value_out[:, where] = piece[:, HD:]


def on_device(
    lines,
    groups,
    parts,
    query_window,
    key_cache,
    value_cache,
    out_weight,
    grad_routed,
    token_route,
    window_start,
):
    window, local_heads = query_window.shape[0], query_window.shape[1] // HD
    half, span, rows = window // lines, key_cache.shape[0], grad_routed.shape[0]
    chips = parts // 2
    line, group, part = lax.axis_index("zh"), lax.axis_index("xy"), lax.axis_index("tp")
    chip, core = part // 2, part % 2
    kv_head = part * local_heads // GROUP
    pieces = [
        ((chip - step + chips) % chips) * 2 + (core + other) % 2
        for step in range(chips)
        for other in range(2)
    ]
    place = jnp.stack(
        [
            line,
            (line * groups + group) * span,
            ((1 - line) * groups + group) * span,
            window_start[0],
            kv_head,
            core,
        ]
        + pieces
    ).astype(jnp.int32)

    route = token_route.reshape(1, window)

    def to_pair(value):
        return lax.ppermute(value, "zh", [(0, 1), (1, 0)])

    def to_core(value):
        return lax.ppermute(value, "tp", [(i, i ^ 1) for i in range(parts)])

    def to_chip(value, step):
        return lax.ppermute(value, "tp", [(i, (i + 2 * step) % parts) for i in range(parts)])

    score_cost = pl.CostEstimate(
        flops=2 * local_heads * span * half * HD,
        bytes_accessed=4 * local_heads * span * half,
        transcendentals=local_heads * span * half,
    )
    score_outs = [
        ((local_heads, span, half), F32),
        ((local_heads, half), F32),
        ((local_heads, half), F32),
    ]
    expo_own, peak_own, total_own, weight, queries = call(
        own_kernel,
        "own_scores",
        (place, route, in_hbm(query_window), in_hbm(key_cache), in_hbm(out_weight)),
        score_outs + [(out_weight.shape, BF), ((half, local_heads * HD), BF)],
        scratch=[
            pltpu.VMEM(query_window.shape, BF),
            pltpu.VMEM((span, HD), BF),
            pltpu.SemaphoreType.DMA((3,)),
        ],
        cost=score_cost,
        streamed=(2, 3, 4),
        held=(0, 3),
    )
    with jax.named_scope("gradient_rows"):
        core_rows = to_core(grad_routed)
        core_rows, weight = lax.optimization_barrier((core_rows, weight))
        chip_rows = jnp.stack([grad_routed, core_rows])
        all_rows = [chip_rows] + [to_chip(chip_rows, step) for step in range(1, chips)]
    with jax.named_scope("cache_pair"):
        mine = jnp.where(
            core == 0,
            lax.dynamic_slice_in_dim(key_cache, kv_head * HD, HD, 1),
            lax.dynamic_slice_in_dim(value_cache, kv_head * HD, HD, 1),
        )
        straight, _ = lax.optimization_barrier((to_pair(mine), peak_own))
        crossed = to_core(straight)
    expo_other, peak_other, total_other = call(
        other_kernel,
        "other_scores",
        (place, route, queries, straight, crossed),
        score_outs,
        cost=score_cost,
        held=(0,),
    )
    all_rows, straight, crossed, expo_other, peak_other, total_other = lax.optimization_barrier(
        (all_rows, straight, crossed, expo_other, peak_other, total_other)
    )
    (gathered,) = call(
        project_kernel,
        "project",
        (place, *all_rows, in_vmem(weight)),
        [((groups, rows, local_heads * HD), BF)],
    )
    with jax.named_scope("head_gradients"):
        grads = lax.all_to_all(gathered, "xy", 0, 0).reshape(half, local_heads * HD)
    own = (in_vmem(expo_own), peak_own)
    other = (in_vmem(expo_other), peak_other)
    stats, probs_grad = call(
        delta_kernel,
        "deltas",
        (place, grads, value_cache, straight, crossed)
        + own
        + (total_own,)
        + other
        + (total_other,),
        [
            ((groups, 3, local_heads, half), F32),
            ((local_heads, 2, span, half), F32),
        ],
        held=(1,),
    )
    with jax.named_scope("row_stats"):
        stats = lax.all_to_all(stats, "xy", 0, 0)
    share = span // parts
    query_part, keep, send = call(
        grads_kernel,
        "gradients",
        (place, route, stats, queries, grads, key_cache, straight, crossed, in_vmem(probs_grad))
        + own
        + other,
        [
            ((groups, lines * rows, local_heads * HD), BF),
            ((2, chips, share, 2 * HD), F32),
            ((2, chips, share, 2 * HD), BF),
        ],
        scratch=[
            pltpu.VMEM((2, local_heads, half), F32),
            pltpu.VMEM((local_heads, half), F32),
            pltpu.VMEM((2, HD, span), BF),
            pltpu.VMEM((2, span, HD), F32),
            pltpu.VMEM((2, span, HD), F32),
        ],
    )
    query_terms = lax.all_to_all(query_part, "xy", 0, 0)
    with jax.named_scope("cache_terms"):
        chip_sum = keep + to_core(send).astype(F32)
        line_sum = chip_sum[0] + to_pair(chip_sum[1].astype(BF)).astype(F32)
        line_sum = line_sum.astype(BF)
        row_shape = (rows, local_heads * HD)
        kept, sent = call(
            query_kernel, "query_sums", (place, query_terms), [(row_shape, F32), (row_shape, BF)]
        )
        line_sum, sent = lax.optimization_barrier((line_sum, sent))
        came = to_pair(sent)
        own = lax.dynamic_index_in_dim(line_sum, chip, 0, False)
        arrived = [own] + [
            to_chip(lax.dynamic_index_in_dim(line_sum, (chip + step) % chips, 0, False), step)
            for step in range(1, chips)
        ]
    width = KVH * HD
    return call(
        finish_kernel,
        "finish",
        (place, kept, came, *arrived),
        [(row_shape, BF), ((share, width), BF), ((share, width), BF)],
    )


def solution(mesh):
    lines = 2
    groups, parts = mesh.shape["ctx"] // lines, mesh.shape["tp"]
    fine = Mesh(mesh.devices.reshape(lines, groups, parts), ("zh", "xy", "tp"))
    ctx = ("zh", "xy")
    in_specs = (
        P(None, "tp"),
        P(ctx, None),
        P(ctx, None),
        P("tp", None),
        P(ctx, "tp"),
        P(),
        P(),
    )
    out_specs = (P(ctx, "tp"), P(ctx + ("tp",), None), P(ctx + ("tp",), None))
    return jax.shard_map(
        functools.partial(on_device, lines, groups, parts),
        mesh=fine,
        in_specs=in_specs,
        out_specs=out_specs,
        check_vma=False,
    )
```

```python
import functools
import math

import jax
import jax.numpy as jnp
from jax import lax
from jax.experimental import pallas as pl
from jax.experimental.pallas import tpu as pltpu
from jax.sharding import Mesh
from jax.sharding import PartitionSpec as P

HQ = 64
KVH = 4
HD = 128
GROUP = HQ // KVH
SCALE = 1.0 / math.sqrt(HD)
NEG = -1e30
FLOOR = -1e29
VMEM_MIB = 16
LOG2E = math.log2(math.e)

BF = jnp.bfloat16
F32 = jnp.float32
ROWS = (((1,), (1,)), ((), ()))


def dot(a, b, dims=None):
    if dims is None:
        return jnp.dot(a, b, preferred_element_type=F32)
    return lax.dot_general(a, b, dims, preferred_element_type=F32)


VMEM = pl.BlockSpec(memory_space=pltpu.VMEM)
SMEM = pl.BlockSpec(memory_space=pltpu.SMEM)


HBM = pl.BlockSpec(memory_space=pltpu.HBM)


def call(kernel, name, args, outs, scratch=(), cost=None, streamed=(), held=()):
    return pl.pallas_call(
        kernel,
        in_specs=[SMEM] + [HBM if i in streamed else VMEM for i in range(1, len(args))],
        out_specs=[VMEM] * len(outs),
        out_shape=[
            pltpu.VMEM(*out) if i in held else jax.ShapeDtypeStruct(*out)
            for i, out in enumerate(outs)
        ],
        scratch_shapes=list(scratch),
        compiler_params=pltpu.CompilerParams(vmem_limit_bytes=VMEM_MIB * 1024 * 1024),
        cost_estimate=cost,
        name=name,
    )(*args)


def in_hbm(array):
    return pltpu.with_memory_space_constraint(array, pltpu.HBM)


def in_vmem(array):
    return pltpu.with_memory_space_constraint(array, pltpu.VMEM)


LINE, FIRST, FIRST_OTHER, START, KV_HEAD, CORE, BLOCKS = range(7)


def columns(index, width=HD):
    return pl.ds(pl.multiple_of(index * width, width), width)


def project_kernel(place, *refs):
    pieces, weight_ref, out_ref = refs[:-2], refs[-2], refs[-1]
    cores, lines, rows, width = pieces[0].shape
    total = None
    for index in range(len(pieces) * cores):
        piece = pieces[index // cores][index % cores].reshape(lines * rows, width)
        term = dot(weight_ref[:, columns(place[BLOCKS + index], width)], piece, ROWS)
        total = term if total is None else total + term
    result = total.T.astype(BF)
    for copy in range(out_ref.shape[0]):
        out_ref[copy] = result


def other_pair(place, straight, crossed):
    swap = place[CORE] == 1
    first, second = straight[...], crossed[...]
    return jnp.where(swap, second, first), jnp.where(swap, first, second)


def score_heads(place, slot, first_row, query_ref, keys, expo_ref, peak_ref, total_ref):
    heads, span, window = expo_ref.shape
    query_pos = place[START] + place[LINE] * window + lax.broadcasted_iota(jnp.int32, (1, window), 1)
    key_pos = place[FIRST + slot] + lax.broadcasted_iota(jnp.int32, (span, 1), 0)

    def one_head(head, _):
        query = query_ref[pl.ds(first_row, window), columns(head)]
        scored = dot(keys, query, ROWS) * (SCALE * LOG2E)
        scored = jnp.where(key_pos <= query_pos, scored, NEG)
        peak = jnp.maximum(jnp.max(scored, axis=0, keepdims=True), FLOOR)
        expo = jnp.exp2(scored - peak)
        expo_ref[head] = expo
        peak_ref[pl.ds(head, 1), :] = peak
        total_ref[pl.ds(head, 1), :] = jnp.sum(expo, axis=0, keepdims=True)
        return 0

    lax.fori_loop(0, heads, one_head, 0, unroll=True)


def own_kernel(
    place,
    query_in,
    key_in,
    weight_in,
    expo_ref,
    peak_ref,
    total_ref,
    weight_out,
    query_ref,
    key_ref,
    loaded,
):
    window = query_ref.shape[0]
    rows = pl.ds(pl.multiple_of(place[LINE] * window, window), window)
    copies = [
        pltpu.make_async_copy(query_in.at[rows], query_ref, loaded.at[0]),
        pltpu.make_async_copy(key_in.at[:, columns(place[KV_HEAD])], key_ref, loaded.at[1]),
        pltpu.make_async_copy(weight_in, weight_out, loaded.at[2]),
    ]
    for copy in copies:
        copy.start()
    copies[0].wait()
    copies[1].wait()
    score_heads(place, 0, 0, query_ref, key_ref[...], expo_ref, peak_ref, total_ref)
    copies[2].wait()


def other_kernel(place, query_ref, straight, crossed, expo_ref, peak_ref, total_ref):
    keys = other_pair(place, straight, crossed)[0]
    window = expo_ref.shape[2]
    first_row = pl.multiple_of(place[LINE] * window, window)
    score_heads(place, 1, first_row, query_ref, keys, expo_ref, peak_ref, total_ref)


def delta_kernel(
    place,
    route_ref,
    gathered_ref,
    value_ref,
    straight,
    crossed,
    expo_own,
    peak_own,
    total_own,
    expo_other,
    peak_other,
    total_other,
    grad_ref,
    stats_ref,
    probs_grad_ref,
):
    heads, span, half = expo_own.shape
    groups, rows, width = gathered_ref.shape
    rows //= 2
    values = (value_ref[:, columns(place[KV_HEAD])], other_pair(place, straight, crossed)[1])
    token = place[LINE] * half + lax.broadcasted_iota(jnp.int32, (half, groups * rows), 0)
    grad = None
    for part, line in enumerate((place[LINE], 1 - place[LINE])):
        pick = route_ref[:, columns(line, groups * rows)] == token
        routed = gathered_ref[:, part * rows : (part + 1) * rows].reshape(groups * rows, width)
        term = dot(jnp.where(pick, 1.0, 0.0).astype(BF), routed)
        grad = term if grad is None else grad + term
    grad_ref[...] = grad.astype(BF)
    peak = jnp.maximum(peak_own[...], peak_other[...])
    factors = (jnp.exp2(peak_own[...] - peak), jnp.exp2(peak_other[...] - peak))
    stats_ref[0, 0] = peak
    stats_ref[0, 1] = total_own[...] * factors[0] + total_other[...] * factors[1]

    def one_head(head, _):
        grad = grad_ref[:, columns(head)]
        for slot, expo_ref in enumerate((expo_own, expo_other)):
            grad_probs = dot(values[slot], grad, ROWS)
            probs_grad_ref[head, slot] = grad_probs
            stats_ref[1 + slot, 2, pl.ds(head, 1), :] = jnp.sum(
                expo_ref[head] * grad_probs, axis=0, keepdims=True
            )
        return 0

    lax.fori_loop(0, heads, one_head, 0, unroll=True)
    stats_ref[0, 2] = stats_ref[1, 2] * factors[0] + stats_ref[2, 2] * factors[1]
    for copy in range(1, stats_ref.shape[0]):
        stats_ref[copy] = stats_ref[0]


def grads_kernel(
    place,
    stats_ref,
    query_ref,
    grad_ref,
    key_ref,
    straight,
    crossed,
    probs_grad_ref,
    expo_own,
    peak_own,
    expo_other,
    peak_other,
    query_out,
    keep_out,
    send_out,
    factor,
    delta,
    keys_turned,
    key_total,
    value_total,
):
    heads, span, half = expo_own.shape
    peaks = stats_ref[:, 0]
    peak = jnp.max(peaks, axis=0)
    weight = jnp.exp2(peaks - peak[None])
    total = jnp.sum(weight * stats_ref[:, 1], axis=0)
    for slot, own_peak in enumerate((peak_own, peak_other)):
        factor[slot] = jnp.exp2(own_peak[...] - peak) / total
    delta[...] = jnp.sum(weight * stats_ref[:, 2], axis=0) / total
    keys = (key_ref[:, columns(place[KV_HEAD])], other_pair(place, straight, crossed)[0])
    for slot in range(2):
        keys_turned[slot] = keys[slot].astype(F32).T.astype(BF)
    key_total[...] = jnp.zeros_like(key_total)
    value_total[...] = jnp.zeros_like(value_total)

    def one_head(head, _):
        query = query_ref[pl.ds(place[LINE] * half, half), columns(head)]
        grad = grad_ref[:, columns(head)]
        row_delta = delta[pl.ds(head, 1), :]
        turned = jnp.zeros((HD, half), F32)
        for slot in range(2):
            expo_ref = (expo_own, expo_other)[slot]
            probs = expo_ref[head] * factor[slot, pl.ds(head, 1), :]
            score_grad = (probs * (probs_grad_ref[head, slot] - row_delta)).astype(BF)
            value_total[slot] += dot(probs.astype(BF), grad)
            key_total[slot] += dot(score_grad, query)
            turned += dot(keys_turned[slot], score_grad)
        result = (SCALE * turned).T.astype(BF)
        query_out[:, :, columns(head)] = result.reshape(query_out.shape[0], query_out.shape[1], HD)
        return 0

    lax.fori_loop(0, heads, one_head, 0, unroll=True)
    slots, chips, share, _ = keep_out.shape
    for slot in range(2):
        for chip in range(chips):
            for part, sums, scale in ((0, key_total, SCALE), (1, value_total, 1.0)):
                where = slice(part * HD, (part + 1) * HD)
                mine = pl.multiple_of((2 * chip + place[CORE]) * share, share)
                theirs = pl.multiple_of((2 * chip + 1 - place[CORE]) * share, share)
                keep_out[slot, chip, :, where] = scale * sums[slot, pl.ds(mine, share), :]
                send_out[slot, chip, :, where] = (
                    scale * sums[slot, pl.ds(theirs, share), :]
                ).astype(BF)


def finish_kernel(place, terms_ref, *refs):
    pieces, (query_out, key_out, value_out) = refs[:-3], refs[-3:]
    query_out[...] = jnp.sum(terms_ref[...].astype(F32), axis=0).astype(BF)
    for step, piece in enumerate(pieces):
        where = columns(place[BLOCKS + 2 * step] // 2)
        key_out[:, where] = piece[:, :HD]
        value_out[:, where] = piece[:, HD:]


def on_device(
    lines,
    groups,
    parts,
    query_window,
    key_cache,
    value_cache,
    out_weight,
    grad_routed,
    token_route,
    window_start,
):
    window, local_heads = query_window.shape[0], query_window.shape[1] // HD
    half, span, rows = window // lines, key_cache.shape[0], grad_routed.shape[0]
    chips = parts // 2
    line, group, part = lax.axis_index("zh"), lax.axis_index("xy"), lax.axis_index("tp")
    chip, core = part // 2, part % 2
    kv_head = part * local_heads // GROUP
    pieces = [
        ((chip - step + chips) % chips) * 2 + (core + other) % 2
        for step in range(chips)
        for other in range(2)
    ]
    place = jnp.stack(
        [
            line,
            (line * groups + group) * span,
            ((1 - line) * groups + group) * span,
            window_start[0],
            kv_head,
            core,
        ]
        + pieces
    ).astype(jnp.int32)

    route = token_route.reshape(1, window)

    def to_pair(value):
        return lax.ppermute(value, "zh", [(0, 1), (1, 0)])

    def to_core(value):
        return lax.ppermute(value, "tp", [(i, i ^ 1) for i in range(parts)])

    def to_chip(value, step):
        return lax.ppermute(value, "tp", [(i, (i + 2 * step) % parts) for i in range(parts)])

    score_cost = pl.CostEstimate(
        flops=2 * local_heads * span * half * HD,
        bytes_accessed=4 * local_heads * span * half,
        transcendentals=local_heads * span * half,
    )
    score_outs = [
        ((local_heads, span, half), F32),
        ((local_heads, half), F32),
        ((local_heads, half), F32),
    ]
    expo_own, peak_own, total_own, weight = call(
        own_kernel,
        "own_scores",
        (place, in_hbm(query_window), in_hbm(key_cache), in_hbm(out_weight)),
        score_outs + [(out_weight.shape, BF)],
        scratch=[
            pltpu.VMEM((half, local_heads * HD), BF),
            pltpu.VMEM((span, HD), BF),
            pltpu.SemaphoreType.DMA((3,)),
        ],
        cost=score_cost,
        streamed=(1, 2, 3),
        held=(0, 3),
    )
    with jax.named_scope("cache_pair"):
        mine = jnp.where(
            core == 0,
            lax.dynamic_slice_in_dim(key_cache, kv_head * HD, HD, 1),
            lax.dynamic_slice_in_dim(value_cache, kv_head * HD, HD, 1),
        )
        straight = to_pair(mine)
    with jax.named_scope("gradient_rows"):
        other_rows = to_pair(grad_routed)
        other_rows, straight, weight = lax.optimization_barrier((other_rows, straight, weight))
        crossed = to_core(straight)
        pair = jnp.stack([grad_routed, other_rows])
        chip_rows = jnp.stack([pair, to_core(pair)])
        all_rows = [chip_rows] + [to_chip(chip_rows, step) for step in range(1, chips)]
    expo_other, peak_other, total_other = call(
        other_kernel,
        "other_scores",
        (place, query_window, straight, crossed),
        score_outs,
        cost=score_cost,
        held=(0,),
    )
    all_rows, straight, crossed, expo_other, peak_other, total_other = lax.optimization_barrier(
        (all_rows, straight, crossed, expo_other, peak_other, total_other)
    )
    (gathered,) = call(
        project_kernel,
        "project",
        (place, *all_rows, in_vmem(weight)),
        [((groups, lines * rows, local_heads * HD), BF)],
    )
    with jax.named_scope("head_gradients"):
        gathered = lax.all_to_all(gathered, "xy", 0, 0)
    own = (in_vmem(expo_own), peak_own)
    other = (in_vmem(expo_other), peak_other)
    grads, stats, probs_grad = call(
        delta_kernel,
        "deltas",
        (place, route, gathered, value_cache, straight, crossed)
        + own
        + (total_own,)
        + other
        + (total_other,),
        [
            ((half, local_heads * HD), BF),
            ((groups, 3, local_heads, half), F32),
            ((local_heads, 2, span, half), F32),
        ],
        held=(2,),
    )
    with jax.named_scope("row_stats"):
        stats = lax.all_to_all(stats, "xy", 0, 0)
    share = span // parts
    query_part, keep, send = call(
        grads_kernel,
        "gradients",
        (place, stats, query_window, grads, key_cache, straight, crossed, in_vmem(probs_grad)) + own + other,
        [
            ((groups, half // groups, local_heads * HD), BF),
            ((2, chips, share, 2 * HD), F32),
            ((2, chips, share, 2 * HD), BF),
        ],
        scratch=[
            pltpu.VMEM((2, local_heads, half), F32),
            pltpu.VMEM((local_heads, half), F32),
            pltpu.VMEM((2, HD, span), BF),
            pltpu.VMEM((2, span, HD), F32),
            pltpu.VMEM((2, span, HD), F32),
        ],
    )
    query_terms = lax.all_to_all(query_part, "xy", 0, 0)
    with jax.named_scope("cache_terms"):
        chip_sum = keep + to_core(send).astype(F32)
        line_sum = chip_sum[0] + to_pair(chip_sum[1].astype(BF)).astype(F32)
        line_sum = line_sum.astype(BF)
        own = lax.dynamic_index_in_dim(line_sum, chip, 0, False)
        arrived = [own] + [
            to_chip(lax.dynamic_index_in_dim(line_sum, (chip + step) % chips, 0, False), step)
            for step in range(1, chips)
        ]
    query_terms, *arrived = lax.optimization_barrier((query_terms, *arrived))
    width = KVH * HD
    return call(
        finish_kernel,
        "finish",
        (place, query_terms, *arrived),
        [
            (query_terms.shape[1:], BF),
            ((share, width), BF),
            ((share, width), BF),
        ],
    )


def solution(mesh):
    lines = 2
    groups, parts = mesh.shape["ctx"] // lines, mesh.shape["tp"]
    fine = Mesh(mesh.devices.reshape(lines, groups, parts), ("zh", "xy", "tp"))
    ctx = ("zh", "xy")
    in_specs = (
        P(None, "tp"),
        P(ctx, None),
        P(ctx, None),
        P("tp", None),
        P(ctx, "tp"),
        P(),
        P(),
    )
    out_specs = (P(ctx, "tp"), P(ctx + ("tp",), None), P(ctx + ("tp",), None))
    return jax.shard_map(
        functools.partial(on_device, lines, groups, parts),
        mesh=fine,
        in_specs=in_specs,
        out_specs=out_specs,
        check_vma=False,
    )
```

```python
import functools
import math

import jax
import jax.numpy as jnp
from jax import lax
from jax.experimental import pallas as pl
from jax.experimental.pallas import tpu as pltpu
from jax.sharding import Mesh
from jax.sharding import PartitionSpec as P

HQ = 64
KVH = 4
HD = 128
GROUP = HQ // KVH
SCALE = 1.0 / math.sqrt(HD)
NEG = -1e30
FLOOR = -1e29
VMEM_MIB = 16
LOG2E = math.log2(math.e)

BF = jnp.bfloat16
F32 = jnp.float32
ROWS = (((1,), (1,)), ((), ()))


def dot(a, b, dims=None):
    if dims is None:
        return jnp.dot(a, b, preferred_element_type=F32)
    return lax.dot_general(a, b, dims, preferred_element_type=F32)


VMEM = pl.BlockSpec(memory_space=pltpu.VMEM)
SMEM = pl.BlockSpec(memory_space=pltpu.SMEM)


HBM = pl.BlockSpec(memory_space=pltpu.HBM)


def call(kernel, name, args, outs, scratch=(), cost=None, streamed=(), held=()):
    return pl.pallas_call(
        kernel,
        in_specs=[SMEM] + [HBM if i in streamed else VMEM for i in range(1, len(args))],
        out_specs=[VMEM] * len(outs),
        out_shape=[
            pltpu.VMEM(*out) if i in held else jax.ShapeDtypeStruct(*out)
            for i, out in enumerate(outs)
        ],
        scratch_shapes=list(scratch),
        compiler_params=pltpu.CompilerParams(vmem_limit_bytes=VMEM_MIB * 1024 * 1024),
        cost_estimate=cost,
        name=name,
    )(*args)


def in_hbm(array):
    return pltpu.with_memory_space_constraint(array, pltpu.HBM)


def in_vmem(array):
    return pltpu.with_memory_space_constraint(array, pltpu.VMEM)


LINE, FIRST, FIRST_OTHER, START, KV_HEAD, CORE, BLOCKS = range(7)


def columns(index, width=HD):
    return pl.ds(pl.multiple_of(index * width, width), width)


def project_pieces(steps, place, pieces, weight_ref):
    total = None
    for step, piece in zip(steps, pieces):
        cores, lines, rows, width = piece.shape
        for core in range(cores):
            block = place[BLOCKS + step * cores + core]
            rows_here = piece[core].reshape(lines * rows, width)
            term = dot(weight_ref[:, columns(block, width)], rows_here, ROWS)
            total = term if total is None else total + term
    return total


def project_first_kernel(steps, place, *refs):
    pieces, weight_ref, partial_ref = refs[:-2], refs[-2], refs[-1]
    partial_ref[...] = project_pieces(steps, place, pieces, weight_ref)


def project_kernel(steps, place, *refs):
    pieces, weight_ref, partial_ref, out_ref = refs[:-3], refs[-3], refs[-2], refs[-1]
    total = partial_ref[...] + project_pieces(steps, place, pieces, weight_ref)
    result = total.T.astype(BF)
    for copy in range(out_ref.shape[0]):
        out_ref[copy] = result


def other_pair(place, straight, crossed):
    swap = place[CORE] == 1
    first, second = straight[...], crossed[...]
    return jnp.where(swap, second, first), jnp.where(swap, first, second)


def score_heads(place, slot, first_row, query_ref, keys, expo_ref, peak_ref, total_ref):
    heads, span, window = expo_ref.shape
    query_pos = place[START] + place[LINE] * window + lax.broadcasted_iota(jnp.int32, (1, window), 1)
    key_pos = place[FIRST + slot] + lax.broadcasted_iota(jnp.int32, (span, 1), 0)

    def one_head(head, _):
        query = query_ref[pl.ds(first_row, window), columns(head)]
        scored = dot(keys, query, ROWS) * (SCALE * LOG2E)
        scored = jnp.where(key_pos <= query_pos, scored, NEG)
        peak = jnp.maximum(jnp.max(scored, axis=0, keepdims=True), FLOOR)
        expo = jnp.exp2(scored - peak)
        expo_ref[head] = expo
        peak_ref[pl.ds(head, 1), :] = peak
        total_ref[pl.ds(head, 1), :] = jnp.sum(expo, axis=0, keepdims=True)
        return 0

    lax.fori_loop(0, heads, one_head, 0, unroll=True)


def own_kernel(
    place,
    query_in,
    key_in,
    weight_in,
    expo_ref,
    peak_ref,
    total_ref,
    weight_out,
    query_ref,
    key_ref,
    loaded,
):
    window = query_ref.shape[0]
    rows = pl.ds(pl.multiple_of(place[LINE] * window, window), window)
    copies = [
        pltpu.make_async_copy(query_in.at[rows], query_ref, loaded.at[0]),
        pltpu.make_async_copy(key_in.at[:, columns(place[KV_HEAD])], key_ref, loaded.at[1]),
        pltpu.make_async_copy(weight_in, weight_out, loaded.at[2]),
    ]
    for copy in copies:
        copy.start()
    copies[0].wait()
    copies[1].wait()
    score_heads(place, 0, 0, query_ref, key_ref[...], expo_ref, peak_ref, total_ref)
    copies[2].wait()


def other_kernel(place, query_ref, straight, crossed, expo_ref, peak_ref, total_ref):
    keys = other_pair(place, straight, crossed)[0]
    window = expo_ref.shape[2]
    first_row = pl.multiple_of(place[LINE] * window, window)
    score_heads(place, 1, first_row, query_ref, keys, expo_ref, peak_ref, total_ref)


def delta_kernel(
    place,
    route_ref,
    gathered_ref,
    value_ref,
    straight,
    crossed,
    expo_own,
    peak_own,
    total_own,
    expo_other,
    peak_other,
    total_other,
    grad_ref,
    stats_ref,
    probs_grad_ref,
):
    heads, span, half = expo_own.shape
    groups, rows, width = gathered_ref.shape
    rows //= 2
    values = (value_ref[:, columns(place[KV_HEAD])], other_pair(place, straight, crossed)[1])
    token = place[LINE] * half + lax.broadcasted_iota(jnp.int32, (half, groups * rows), 0)
    grad = None
    for part, line in enumerate((place[LINE], 1 - place[LINE])):
        pick = route_ref[:, columns(line, groups * rows)] == token
        routed = gathered_ref[:, part * rows : (part + 1) * rows].reshape(groups * rows, width)
        term = dot(jnp.where(pick, 1.0, 0.0).astype(BF), routed)
        grad = term if grad is None else grad + term
    grad_ref[...] = grad.astype(BF)
    peak = jnp.maximum(peak_own[...], peak_other[...])
    factors = (jnp.exp2(peak_own[...] - peak), jnp.exp2(peak_other[...] - peak))
    stats_ref[0, 0] = peak
    stats_ref[0, 1] = total_own[...] * factors[0] + total_other[...] * factors[1]

    def one_head(head, _):
        grad = grad_ref[:, columns(head)]
        for slot, expo_ref in enumerate((expo_own, expo_other)):
            grad_probs = dot(values[slot], grad, ROWS)
            probs_grad_ref[head, slot] = grad_probs
            stats_ref[1 + slot, 2, pl.ds(head, 1), :] = jnp.sum(
                expo_ref[head] * grad_probs, axis=0, keepdims=True
            )
        return 0

    lax.fori_loop(0, heads, one_head, 0, unroll=True)
    stats_ref[0, 2] = stats_ref[1, 2] * factors[0] + stats_ref[2, 2] * factors[1]
    for copy in range(1, stats_ref.shape[0]):
        stats_ref[copy] = stats_ref[0]


def grads_kernel(
    place,
    stats_ref,
    query_ref,
    grad_ref,
    key_ref,
    straight,
    crossed,
    probs_grad_ref,
    expo_own,
    peak_own,
    expo_other,
    peak_other,
    query_out,
    keep_out,
    send_out,
    factor,
    delta,
    keys_turned,
    key_total,
    value_total,
):
    heads, span, half = expo_own.shape
    peaks = stats_ref[:, 0]
    peak = jnp.max(peaks, axis=0)
    weight = jnp.exp2(peaks - peak[None])
    total = jnp.sum(weight * stats_ref[:, 1], axis=0)
    for slot, own_peak in enumerate((peak_own, peak_other)):
        factor[slot] = jnp.exp2(own_peak[...] - peak) / total
    delta[...] = jnp.sum(weight * stats_ref[:, 2], axis=0) / total
    keys = (key_ref[:, columns(place[KV_HEAD])], other_pair(place, straight, crossed)[0])
    for slot in range(2):
        keys_turned[slot] = keys[slot].astype(F32).T.astype(BF)
    key_total[...] = jnp.zeros_like(key_total)
    value_total[...] = jnp.zeros_like(value_total)

    def one_head(head, _):
        query = query_ref[pl.ds(place[LINE] * half, half), columns(head)]
        grad = grad_ref[:, columns(head)]
        row_delta = delta[pl.ds(head, 1), :]
        turned = jnp.zeros((HD, half), F32)
        for slot in range(2):
            expo_ref = (expo_own, expo_other)[slot]
            probs = expo_ref[head] * factor[slot, pl.ds(head, 1), :]
            score_grad = (probs * (probs_grad_ref[head, slot] - row_delta)).astype(BF)
            value_total[slot] += dot(probs.astype(BF), grad)
            key_total[slot] += dot(score_grad, query)
            turned += dot(keys_turned[slot], score_grad)
        result = (SCALE * turned).T.astype(BF)
        query_out[:, :, columns(head)] = result.reshape(query_out.shape[0], query_out.shape[1], HD)
        return 0

    lax.fori_loop(0, heads, one_head, 0, unroll=True)
    slots, chips, share, _ = keep_out.shape
    for slot in range(2):
        for chip in range(chips):
            for part, sums, scale in ((0, key_total, SCALE), (1, value_total, 1.0)):
                where = slice(part * HD, (part + 1) * HD)
                mine = pl.multiple_of((2 * chip + place[CORE]) * share, share)
                theirs = pl.multiple_of((2 * chip + 1 - place[CORE]) * share, share)
                keep_out[slot, chip, :, where] = scale * sums[slot, pl.ds(mine, share), :]
                send_out[slot, chip, :, where] = (
                    scale * sums[slot, pl.ds(theirs, share), :]
                ).astype(BF)


def finish_kernel(place, terms_ref, *refs):
    pieces, (query_out, key_out, value_out) = refs[:-3], refs[-3:]
    query_out[...] = jnp.sum(terms_ref[...].astype(F32), axis=0).astype(BF)
    for step, piece in enumerate(pieces):
        where = columns(place[BLOCKS + 2 * step] // 2)
        key_out[:, where] = piece[:, :HD]
        value_out[:, where] = piece[:, HD:]


def on_device(
    lines,
    groups,
    parts,
    query_window,
    key_cache,
    value_cache,
    out_weight,
    grad_routed,
    token_route,
    window_start,
):
    window, local_heads = query_window.shape[0], query_window.shape[1] // HD
    half, span, rows = window // lines, key_cache.shape[0], grad_routed.shape[0]
    chips = parts // 2
    line, group, part = lax.axis_index("zh"), lax.axis_index("xy"), lax.axis_index("tp")
    chip, core = part // 2, part % 2
    kv_head = part * local_heads // GROUP
    pieces = [
        ((chip - step + chips) % chips) * 2 + (core + other) % 2
        for step in range(chips)
        for other in range(2)
    ]
    place = jnp.stack(
        [
            line,
            (line * groups + group) * span,
            ((1 - line) * groups + group) * span,
            window_start[0],
            kv_head,
            core,
        ]
        + pieces
    ).astype(jnp.int32)

    route = token_route.reshape(1, window)

    def to_pair(value):
        return lax.ppermute(value, "zh", [(0, 1), (1, 0)])

    def to_core(value):
        return lax.ppermute(value, "tp", [(i, i ^ 1) for i in range(parts)])

    def to_chip(value, step):
        return lax.ppermute(value, "tp", [(i, (i + 2 * step) % parts) for i in range(parts)])

    score_cost = pl.CostEstimate(
        flops=2 * local_heads * span * half * HD,
        bytes_accessed=4 * local_heads * span * half,
        transcendentals=local_heads * span * half,
    )
    score_outs = [
        ((local_heads, span, half), F32),
        ((local_heads, half), F32),
        ((local_heads, half), F32),
    ]
    expo_own, peak_own, total_own, weight = call(
        own_kernel,
        "own_scores",
        (place, in_hbm(query_window), in_hbm(key_cache), in_hbm(out_weight)),
        score_outs + [(out_weight.shape, BF)],
        scratch=[
            pltpu.VMEM((half, local_heads * HD), BF),
            pltpu.VMEM((span, HD), BF),
            pltpu.SemaphoreType.DMA((3,)),
        ],
        cost=score_cost,
        streamed=(1, 2, 3),
        held=(0, 3),
    )
    with jax.named_scope("cache_pair"):
        mine = jnp.where(
            core == 0,
            lax.dynamic_slice_in_dim(key_cache, kv_head * HD, HD, 1),
            lax.dynamic_slice_in_dim(value_cache, kv_head * HD, HD, 1),
        )
        straight = to_pair(mine)
    with jax.named_scope("gradient_rows"):
        other_rows = to_pair(grad_routed)
        other_rows, straight, weight = lax.optimization_barrier((other_rows, straight, weight))
        crossed = to_core(straight)
        pair = jnp.stack([grad_routed, other_rows])
        chip_rows = jnp.stack([pair, to_core(pair)])
        all_rows = [chip_rows] + [to_chip(chip_rows, step) for step in range(1, chips)]
    expo_other, peak_other, total_other = call(
        other_kernel,
        "other_scores",
        (place, query_window, straight, crossed),
        score_outs,
        cost=score_cost,
        held=(0,),
    )
    early, late = (0, chips - 1), tuple(range(1, chips - 1))
    (partial,) = call(
        functools.partial(project_first_kernel, early),
        "project_first",
        (place, *[all_rows[step] for step in early], in_vmem(weight)),
        [((local_heads * HD, lines * rows), F32)],
        cost=score_cost,
    )
    late_rows = [all_rows[step] for step in late]
    late_rows, partial, straight, crossed, expo_other, peak_other, total_other = (
        lax.optimization_barrier(
            (late_rows, partial, straight, crossed, expo_other, peak_other, total_other)
        )
    )
    (gathered,) = call(
        functools.partial(project_kernel, late),
        "project",
        (place, *late_rows, in_vmem(weight), partial),
        [((groups, lines * rows, local_heads * HD), BF)],
    )
    with jax.named_scope("head_gradients"):
        gathered = lax.all_to_all(gathered, "xy", 0, 0)
    own = (in_vmem(expo_own), peak_own)
    other = (in_vmem(expo_other), peak_other)
    grads, stats, probs_grad = call(
        delta_kernel,
        "deltas",
        (place, route, gathered, value_cache, straight, crossed)
        + own
        + (total_own,)
        + other
        + (total_other,),
        [
            ((half, local_heads * HD), BF),
            ((groups, 3, local_heads, half), F32),
            ((local_heads, 2, span, half), F32),
        ],
        held=(2,),
    )
    with jax.named_scope("row_stats"):
        stats = lax.all_to_all(stats, "xy", 0, 0)
    share = span // parts
    query_part, keep, send = call(
        grads_kernel,
        "gradients",
        (place, stats, query_window, grads, key_cache, straight, crossed, in_vmem(probs_grad)) + own + other,
        [
            ((groups, half // groups, local_heads * HD), BF),
            ((2, chips, share, 2 * HD), F32),
            ((2, chips, share, 2 * HD), BF),
        ],
        scratch=[
            pltpu.VMEM((2, local_heads, half), F32),
            pltpu.VMEM((local_heads, half), F32),
            pltpu.VMEM((2, HD, span), BF),
            pltpu.VMEM((2, span, HD), F32),
            pltpu.VMEM((2, span, HD), F32),
        ],
    )
    query_terms = lax.all_to_all(query_part, "xy", 0, 0)
    with jax.named_scope("cache_terms"):
        chip_sum = keep + to_core(send).astype(F32)
        line_sum = chip_sum[0] + to_pair(chip_sum[1].astype(BF)).astype(F32)
        line_sum = line_sum.astype(BF)
        own = lax.dynamic_index_in_dim(line_sum, chip, 0, False)
        arrived = [own] + [
            to_chip(lax.dynamic_index_in_dim(line_sum, (chip + step) % chips, 0, False), step)
            for step in range(1, chips)
        ]
    query_terms, *arrived = lax.optimization_barrier((query_terms, *arrived))
    width = KVH * HD
    return call(
        finish_kernel,
        "finish",
        (place, query_terms, *arrived),
        [
            (query_terms.shape[1:], BF),
            ((share, width), BF),
            ((share, width), BF),
        ],
    )


def solution(mesh):
    lines = 2
    groups, parts = mesh.shape["ctx"] // lines, mesh.shape["tp"]
    fine = Mesh(mesh.devices.reshape(lines, groups, parts), ("zh", "xy", "tp"))
    ctx = ("zh", "xy")
    in_specs = (
        P(None, "tp"),
        P(ctx, None),
        P(ctx, None),
        P("tp", None),
        P(ctx, "tp"),
        P(),
        P(),
    )
    out_specs = (P(ctx, "tp"), P(ctx + ("tp",), None), P(ctx + ("tp",), None))
    return jax.shard_map(
        functools.partial(on_device, lines, groups, parts),
        mesh=fine,
        in_specs=in_specs,
        out_specs=out_specs,
        check_vma=False,
    )
```
